256 devices in a mesh: tm: 64 (over z, x, core), space: 4 (over y).
Axes of the slice: x: 4, y: 4, z: 8, core: 2. Of those that a mesh axis runs over, the one named last changes fastest.
Arguments:
- frames: bfloat16 [256, 32, 256, 128], P('tm', 'space'), may hold values from -8 to 8
- conv_weight: bfloat16 [3, 1152, 128], replicated, may hold values from -0.109375 to 0.109375
- norm_gain: float32 [128], replicated, may hold values from 0.1 to 1.9
- norm_shift: float32 [128], replicated, may hold values from -3 to 3
- clip_lengths: int32 [32], replicated, may hold values from 1 to 64, 256 in all
Outputs:
- encoded: bfloat16 [256, 32, 256, 128], P('tm', 'space')
The draws below stay inside these ranges and needn't reach their ends.
Inputs may be any that keep to these rules, and one draw needn't show every extreme that they name: `clip_lengths`: clips are packed end to end and fill all 256 frames; the longest has exactly 64 frames.
All inputs are finite; a program needn't handle non-finite values.
Results may differ from the reference program's by a relative error of at most 0.00065.
Values may be sent and summed in bfloat16 or wider, within the bound.
A program may use at most 192 MiB of HBM per device.

```python
import math
import jax
import jax.numpy as jnp
import numpy as np
from jax import lax

C = 128
GROUPS = 32
WCOL = 256
TOTAL_FRAMES = 256
NROWS = 32
CLIPS = 32
MOST = 64


def draw_frames(key, part):
    key = jax.random.fold_in(key, 11)
    noise_key, common_key, frame_key = jax.random.split(key, 3)
    shape = (TOTAL_FRAMES, NROWS, WCOL, C)
    noise = jax.random.normal(noise_key, shape, jnp.float32)
    common = 0.6 * jax.random.normal(common_key, (C,), jnp.float32)
    per_frame = 0.4 * jax.random.normal(frame_key, (TOTAL_FRAMES, C), jnp.float32)
    values = noise + common[None, None, None, :] + per_frame[:, None, None, :]
    return jnp.clip(values, -8.0, 8.0).astype(jnp.bfloat16)


def length_profile(count, total, bound, lean):
    loads = [(1 << 20) // math.isqrt(rank ** lean) + 1 for rank in range(2, count + 1)]
    spare, given = total - bound - (count - 1), [1] * (count - 1)
    while spare > 0:
        movable = [i for i in range(count - 1) if given[i] < bound]
        whole, left = sum([loads[i] for i in movable]), spare
        for i in movable:
            addition = min(bound - given[i], max(1, left * loads[i] // whole), spare)
            given[i] = given[i] + addition
            spare = spare - addition
    return np.array([bound] + given)


def ragged(rng, amount, total, limit, lean):
    if amount == 2:
        one = jax.random.randint(rng, (), max(1, total - limit), min(limit, total - 1) + 1)
        return jnp.stack([one, total - one])
    sizes = jnp.asarray(length_profile(amount, total, limit, lean), jnp.int32)
    pairs = (amount - 1) // 2
    giver, taker = sizes[1:1 + 2 * pairs:2], sizes[2:2 + 2 * pairs:2]
    slack = jnp.minimum(giver - 1, limit - taker)
    shifted = jax.random.randint(jax.random.fold_in(rng, 1), (pairs,), 0, 1 << 20) % (slack + 1)
    sizes = sizes.at[1:1 + 2 * pairs:2].set(giver - shifted).at[2:2 + 2 * pairs:2].set(taker + shifted)
    return sizes[jax.random.permutation(jax.random.fold_in(rng, 2), amount)]


def scatter_about(own_key, dims, width, most, held_as=jnp.bfloat16):
    result = width * jax.random.normal(own_key, dims, jnp.float32)
    return jnp.clip(result, min=-most, max=most).astype(held_as)


def setup_inputs(seed: int = 0) -> dict:
    streams_of = jax.random.split(jax.random.key(seed), 6)
    frames = draw_frames(jax.random.fold_in(streams_of[5], 71), 0)
    conv_weight = scatter_about(streams_of[1], (3, 9 * C, C), (27 * C) ** -0.5, 0.109375)
    norm_gain = jnp.clip(1.0 + 0.18 * jax.random.normal(streams_of[2], (C,), jnp.float32), 0.1, 1.9)
    norm_shift = scatter_about(streams_of[3], (C,), 0.5, 3.0, jnp.float32)
    clip_lengths = ragged(streams_of[4], CLIPS, TOTAL_FRAMES, MOST, 2).astype(jnp.int32)
    return {"frames": frames, "conv_weight": conv_weight, "norm_gain": norm_gain, "norm_shift": norm_shift, "clip_lengths": clip_lengths}


def patches_of(source, band_rows, columns):
    pieces = []
    for row_off in range(3):
        for col_off in range(3):
            pieces.append(source[row_off:row_off + band_rows, col_off:col_off + columns, :])
    return jnp.concatenate(pieces, axis=-1)

def reference(frames, conv_weight, norm_gain, norm_shift, clip_lengths):
    count_frames, band_rows, columns, channels = frames.shape
    clip_count = clip_lengths.shape[0]
    per_group = channels // GROUPS
    clip_ends = jnp.cumsum(clip_lengths).astype(jnp.int32)
    positions = jnp.arange(count_frames, dtype=jnp.int32)
    clip_of = lax.optimization_barrier(jnp.sum((clip_ends[None, :] <= positions[:, None]).astype(jnp.int32), axis=1)).astype(jnp.int32)
    padded = jnp.pad(frames, ((2, 0), (1, 1), (1, 1), (0, 0)))
    clip_padded = jnp.concatenate([jnp.full((2,), -1, jnp.int32), clip_of]).astype(jnp.int32)

    def one_frame(position):
        running = jnp.zeros((band_rows * columns, channels), jnp.float32)
        for step_back in range(3):
            index = (position + 2 - step_back).astype(jnp.int32)
            source = lax.dynamic_index_in_dim(padded, index, 0, keepdims=False)
            patches = patches_of(source, band_rows, columns).reshape(band_rows * columns, 9 * channels)
            within = (clip_padded[index] == clip_of[position]).astype(jnp.float32)
            running = running + within * jnp.dot(patches, conv_weight[step_back], preferred_element_type=jnp.float32)
        return running.reshape(band_rows, columns, channels)
    conv = lax.map(one_frame, positions)
    onehot = (clip_of[:, None] == jnp.arange(clip_count, dtype=jnp.int32)[None, :]).astype(jnp.float32)
    counts = clip_lengths.astype(jnp.float32) * float(band_rows * columns * per_group)

    def group_stat(values):
        frame_sums = lax.optimization_barrier(jnp.sum(values, axis=(1, 2)))
        clip_sums = jnp.dot(onehot.T, frame_sums, precision=lax.Precision.HIGHEST)
        return lax.optimization_barrier(jnp.sum(clip_sums.reshape(clip_count, GROUPS, per_group), axis=-1)) / counts[:, None]

    def spread(table):
        frame_table = jnp.dot(onehot, table, precision=lax.Precision.HIGHEST)
        return jnp.repeat(frame_table, per_group, axis=1)[:, None, None, :]
    average = group_stat(conv)
    centered = conv - spread(average)
    variance = group_stat(centered * centered)
    normed = centered * spread(lax.rsqrt(variance + 1e-06)) * norm_gain + norm_shift
    return jax.nn.silu(normed).astype(jnp.bfloat16)
```

```python
import functools

import jax
import jax.numpy as jnp
from jax import lax
from jax.experimental import pallas as pl
from jax.experimental.pallas import tpu as pltpu
from jax.sharding import PartitionSpec as P

GROUPS = 32
MESH = pl.DeviceIdType.MESH
T, S, NX, NZ = 64, 4, 4, 8
FR, ROWS, COLS, CH = 4, 8, 256, 128
BF, F32 = jnp.bfloat16, jnp.float32


def shifted(v):
    z = jnp.zeros((1, CH), v.dtype)
    left = jnp.concatenate([z, v[: COLS - 1]], axis=0)
    right = jnp.concatenate([v[1:], z], axis=0)
    return jnp.concatenate([left, v, right], axis=1)


def group_sum(x):
    lane = lax.broadcasted_iota(jnp.int32, x.shape, 1)
    n = x.shape[1]
    x = x + jnp.where(lane % 2 == 0, pltpu.roll(x, n - 1, 1), pltpu.roll(x, 1, 1))
    return x + jnp.where(lane % 4 < 2, pltpu.roll(x, n - 2, 1), pltpu.roll(x, 2, 1))


def conv_kernel(x, w, lens, acc, tab, XL, XH, YU, YD, PA, W, sS, sQ, st, ct, buf1, buf2,
                lsem, wsem, xsem_s, xsem_r, ysem_s, ysem_r, s1_s, s1_r, s2_s, s2_r):
    t = lax.axis_index("tm")
    y = lax.axis_index("space")
    core = t % 2
    chip = t // 2
    cx = chip % NX
    cz = chip // NX

    def dev(z_, x_, c_, y_):
        return ((z_ * NX + x_) * 2 + c_, y_)

    nxt = ((t + 1) % T, y)
    up = (t, (y + 1) % S)
    down = (t, (y + S - 1) % S)

    near = [(dc, dy) for dc in range(2) for dy in range(S) if (dc, dy) != (0, 0)]
    far = [(dz, dx) for dz in (2, -2, 1, -1, 0) for dx in (2, 1, 3, 0) if (dz, dx) != (0, 0)]
    barrier = pltpu.get_barrier_semaphore()

    def greet(d):
        pl.semaphore_signal(barrier, inc=1, device_id=d, device_id_type=MESH)

    greet(((t + 2 * core - 1 + T) % T, y))

    def near_dev(dc, dy):
        return dev(cz, cx, (core + dc) % 2, (y + dy) % S)

    def far_dev(dz, dx):
        return dev((cz + dz + NZ) % NZ, (cx + dx) % NX, core, y)

    for dc, dy in near:
        greet(near_dev(dc, dy))
    for dz, dx in far:
        greet(far_dev(dz, dx))

    loads = [pltpu.make_async_copy(x.at[f], XL.at[f], lsem.at[f]) for f in range(FR)]
    wloads = []
    for lag in range(3):
        wloads.append(pltpu.make_async_copy(w.at[lag], W.at[lag, pl.ds(0, 1152), pl.ds(0, 128)], wsem.at[lag]))
        wloads.append(pltpu.make_async_copy(w.at[lag], W.at[lag, pl.ds(384, 1152), pl.ds(128, 128)], wsem.at[3 + lag]))
    for c in loads + wloads:
        c.start()

    pl.semaphore_wait(barrier, 1 + len(near) + len(far))

    def rcopy(src, dst, ss, rs, d):
        return pltpu.make_async_remote_copy(src_ref=src, dst_ref=dst, send_sem=ss, recv_sem=rs, device_id=d, device_id_type=MESH)

    xc = []
    for i, (r0, n) in enumerate([(0, 1), (7, 1), (1, 2), (3, 2), (5, 2)]):
        xc.append(rcopy(x.at[pl.ds(2, 2), pl.ds(r0, n)], XH.at[:, pl.ds(r0, n)], xsem_s.at[i], xsem_r.at[i], nxt))
    yc = [
        rcopy(x.at[:, 7], YU.at[pl.ds(2, 4)], ysem_s.at[0], ysem_r.at[0], up),
        rcopy(x.at[:, 0], YD.at[pl.ds(2, 4)], ysem_s.at[1], ysem_r.at[1], down),
        rcopy(XH.at[:, 7], YU.at[pl.ds(0, 2)], ysem_s.at[2], ysem_r.at[2], up),
        rcopy(XH.at[:, 0], YD.at[pl.ds(0, 2)], ysem_s.at[3], ysem_r.at[3], down),
    ]
    xc[0].start()
    xc[1].start()
    yc[0].start()
    yc[1].start()
    xc[2].start()
    xc[3].start()
    xc[4].start()

    pos = [t * FR + i for i in range(FR)]

    def bounds(k, c):
        cum, starts, ends = c
        after = cum + lens[k]
        inside = [(cum <= p) & (p < after) for p in pos]
        starts = tuple(jnp.where(i, cum, s) for i, s in zip(inside, starts))
        ends = tuple(jnp.where(i, after, e) for i, e in zip(inside, ends))
        return after, starts, ends

    zero = jnp.int32(0)
    _, starts, ends = lax.fori_loop(0, 32, bounds, (zero, (zero,) * FR, (zero,) * FR))
    within = [[jnp.where(pos[i] - lag >= starts[i], 1.0, 0.0).astype(F32) for lag in range(3)] for i in range(FR)]

    for lag in range(3):
        W[lag, 1152:1536, 0:128] = jnp.zeros((384, 128), BF)
        W[lag, 0:384, 128:256] = jnp.zeros((384, 128), BF)

    for f in range(FR):
        loads[f].wait()

        def pairs(p, _, f=f):
            PA[f + 2, p, :, 0:384] = shifted(XL[f, 2 * p - 1])
            PA[f + 2, p, :, 384:768] = shifted(XL[f, 2 * p])
            return 0

        lax.fori_loop(1, 4, pairs, 0)
        PA[f + 2, 0, :, 384:768] = shifted(XL[f, 0])
        PA[f + 2, 4, :, 0:384] = shifted(XL[f, 7])
    for c in wloads:
        c.wait()

    def dot(a, b):
        return jnp.dot(a, b, preferred_element_type=F32)

    def local(i, lag):
        a = PA[i + 2 - lag, 1:4].reshape(768, 768)
        d1 = dot(a, W[lag, 768:1536]).reshape(3, 256, 256)
        d0 = dot(a, W[lag, 0:768]).reshape(3, 256, 256)
        return d1, d0

    for i in range(FR):
        d1, d0 = local(i, 0)
        acc[i, 0] = d1[0]
        acc[i, 1] = d1[1] + d0[0]
        acc[i, 2] = d1[2] + d0[1]
        acc[i, 3] = d0[2]
        for lag in range(1, min(i, 2) + 1):
            d1, d0 = local(i, lag)
            s = within[i][lag]
            acc[i, 0] += s * d1[0]
            acc[i, 1] += s * (d1[1] + d0[0])
            acc[i, 2] += s * (d1[2] + d0[1])
            acc[i, 3] += s * d0[2]
        if i == 1:
            xc[0].wait_recv()
            xc[1].wait_recv()
            yc[2].start()
            yc[3].start()

    has_up = y > 0
    has_down = y < S - 1
    yc[0].wait_recv()
    yc[1].wait_recv()
    zrow = jnp.zeros((COLS, CH), BF)

    def rims(f, _):
        PA[f, 0, :, 0:384] = shifted(jnp.where(has_up, YU[f], zrow))
        PA[f, 4, :, 384:768] = shifted(jnp.where(has_down, YD[f], zrow))
        return 0

    lax.fori_loop(2, 6, rims, 0)

    def rim_dots(lag, lo):
        n = FR - lo
        a = PA[lo + 2 - lag : FR + 2 - lag, 0].reshape(n * 256, 768)
        d = dot(a, W[lag, 0:768]).reshape(n, 256, 256)
        a2 = PA[lo + 2 - lag : FR + 2 - lag, 4].reshape(n * 256, 768)
        d2 = dot(a2, W[lag, 768:1536]).reshape(n, 256, 256)
        for i in range(lo, FR):
            acc[i, 0] += within[i][lag] * d[i - lo]
            acc[i, 3] += within[i][lag] * d2[i - lo]

    for lag in range(3):
        rim_dots(lag, lag)

    def stat(i, k):
        v = acc[i, k]
        s = jnp.sum(v, axis=0, keepdims=True)
        c = v - s * (1.0 / 256)
        q = jnp.sum(c * c, axis=0, keepdims=True)
        sS[i, pl.ds(k, 1)] = s
        sQ[i, pl.ds(k, 1)] = q

    def stat_loop(n, _):
        stat(2 + n // 4, n % 4)
        return 0

    lax.fori_loop(0, 8, stat_loop, 0)

    def early(p):
        a1 = PA[1, p]
        a2 = PA[0:2, p].reshape(512, 768)
        if p < 4:
            e = dot(a1, W[1, 0:768])
            g = dot(a2, W[2, 0:768])
            acc[0, p] += within[0][1] * e + within[0][2] * g[0:256]
            acc[1, p] += within[1][2] * g[256:512]
        if p > 0:
            e = dot(a1, W[1, 768:1536])
            g = dot(a2, W[2, 768:1536])
            acc[0, p - 1] += within[0][1] * e + within[0][2] * g[0:256]
            acc[1, p - 1] += within[1][2] * g[256:512]

    def early_rows(p):
        for f in range(2):
            PA[f, p, :, 0:384] = shifted(XH[f, 2 * p - 1])
            PA[f, p, :, 384:768] = shifted(XH[f, 2 * p])

    xc[2].wait_recv()
    early_rows(1)
    early(1)
    yc[2].wait_recv()
    yc[3].wait_recv()
    for f in range(2):
        PA[f, 0, :, 384:768] = shifted(XH[f, 0])
        PA[f, 4, :, 0:384] = shifted(XH[f, 7])
    lax.fori_loop(0, 2, rims, 0)
    early(0)
    early(4)
    stat(0, 0)
    stat(1, 0)
    xc[3].wait_recv()
    early_rows(2)
    early(2)
    stat(0, 1)
    stat(1, 1)
    xc[4].wait_recv()
    early_rows(3)
    early(3)
    stat(0, 2)
    stat(1, 2)
    stat(0, 3)
    stat(1, 3)

    means, squares = [], []
    for i in range(FR):
        s = sS[i]
        q = sQ[i]
        m = s * (1.0 / 256)
        tot = jnp.sum(s, axis=0, keepdims=True)
        mean = (tot[:, :128] + tot[:, 128:]) * (1.0 / 2048)
        both = jnp.concatenate([mean, mean], axis=1)
        dm = m - both
        qq = jnp.sum(q + 256.0 * dm * dm, axis=0, keepdims=True)
        means.append(mean)
        squares.append(qq[:, :128] + qq[:, 128:])
    mine = jnp.concatenate(means + squares, axis=0)
    st[...] = mine
    buf1[core * S + y] = mine

    s1 = []
    for i, (dc, dy) in enumerate(near):
        s1.append(rcopy(st, buf1.at[core * S + y], s1_s.at[i], s1_r.at[i], near_dev(dc, dy)))
    for c in s1:
        c.start()
    for c in s1:
        c.wait_recv()

    parts = []
    for c in range(2):
        b = buf1[pl.ds(c * S, S)]
        m = b[:, 0:4]
        mean = jnp.sum(m, axis=0) * (1.0 / S)
        dm = m - mean[None]
        parts.append((mean, jnp.sum(b[:, 4:8] + 2048.0 * dm * dm, axis=0)))
    chip_table = jnp.concatenate([parts[0][0], parts[1][0], parts[0][1], parts[1][1]], axis=0)
    ct[...] = chip_table
    buf2[2 * NX + cx] = chip_table

    s2 = []
    for i, (dz, dx) in enumerate(far):
        s2.append(rcopy(ct, buf2.at[(2 - dz) * NX + cx], s2_s.at[i], s2_r.at[i], far_dev(dz, dx)))
    for c in s2:
        c.start()
    for c in s2:
        c.wait_recv()

    shape = (5 * NX, 8, 128)
    slot = lax.broadcasted_iota(jnp.int32, shape, 0)
    row = lax.broadcasted_iota(jnp.int32, shape, 1)
    frame = ((cz - 2) * NX + slot) * 8 + row
    mean_e = buf2[:, 0:8]
    m2_e = buf2[:, 8:16]
    masks = [((frame >= starts[i]) & (frame < ends[i])).astype(F32) for i in range(FR)]
    lengths = [(ends[i] - starts[i]).astype(F32) for i in range(FR)]
    total = [jnp.sum(jnp.sum(masks[i] * mean_e, axis=0), axis=0, keepdims=True) / (lengths[i] * 4.0) for i in range(FR)]
    avg = group_sum(jnp.concatenate(total + total, axis=0))
    vs = []
    for i in range(FR):
        d = mean_e - avg[i : i + 1][None]
        e = masks[i] * (m2_e + 8192.0 * d * d)
        vs.append(jnp.sum(jnp.sum(e, axis=0), axis=0, keepdims=True) / (lengths[i] * (8192.0 * 4.0)))
    var = group_sum(jnp.concatenate(vs + vs, axis=0))
    rstd = lax.rsqrt(var + 1e-6)
    tab[...] = jnp.concatenate([avg[0:4], rstd[0:4]], axis=0)

    for c in xc + yc + s1 + s2:
        c.wait_send()


def norm_kernel(acc, tab, gain, shift, out):
    i = pl.program_id(0)
    avg = tab[pl.ds(i, 1)]
    scale = tab[pl.ds(i + 4, 1)] * gain[...]
    off = shift[...]
    for k in range(4):
        for h in range(2):
            v = (acc[0, k, :, h * 128 : (h + 1) * 128] - avg) * scale + off
            out[0, 2 * k + h] = (v * (1.0 / (1.0 + jnp.exp(-v)))).astype(BF)


def shards(frames, conv_weight, norm_gain, norm_shift, clip_lengths):
    V = pltpu.VMEM
    D = pltpu.SemaphoreType.DMA
    anyspec = pl.BlockSpec(memory_space=pltpu.HBM)
    vspec = pl.BlockSpec(memory_space=V)
    acc, tab = pl.pallas_call(
        conv_kernel,
        out_shape=(jax.ShapeDtypeStruct((FR, 4, 256, 256), F32), jax.ShapeDtypeStruct((8, 128), F32)),
        in_specs=[anyspec, anyspec, pl.BlockSpec(memory_space=pltpu.SMEM)],
        out_specs=(vspec, vspec),
        scratch_shapes=[
            V((4, 8, 256, 128), BF), V((2, 8, 256, 128), BF), V((6, 256, 128), BF), V((6, 256, 128), BF),
            V((6, 5, 256, 768), BF), V((3, 1536, 256), BF),
            V((4, 4, 256), F32), V((4, 4, 256), F32), V((8, 128), F32), V((16, 128), F32),
            V((8, 8, 128), F32), V((20, 16, 128), F32),
            D((4,)), D((6,)), D((5,)), D((5,)), D((4,)), D((4,)), D((7,)), D((7,)), D((19,)), D((19,)),
        ],
        compiler_params=pltpu.CompilerParams(collective_id=0, has_side_effects=True, vmem_limit_bytes=48 * 2**20),
        name="conv_stats",
    )(frames, conv_weight, clip_lengths)
    return pl.pallas_call(
        norm_kernel,
        grid=(FR,),
        out_shape=jax.ShapeDtypeStruct((FR, ROWS, COLS, CH), BF),
        in_specs=[
            pl.BlockSpec((1, 4, 256, 256), lambda i: (i, 0, 0, 0)),
            pl.BlockSpec((8, 128), lambda i: (0, 0)),
            pl.BlockSpec((1, 128), lambda i: (0, 0)),
            pl.BlockSpec((1, 128), lambda i: (0, 0)),
        ],
        out_specs=pl.BlockSpec((1, ROWS, COLS, CH), lambda i: (i, 0, 0, 0)),
        name="normalize",
    )(acc, tab, norm_gain.reshape(1, CH), norm_shift.reshape(1, CH))


def solution(mesh):
    return jax.shard_map(
        shards,
        mesh=mesh,
        in_specs=(P("tm", "space", None, None), P(), P(), P(), P()),
        out_specs=P("tm", "space", None, None),
        check_vma=False,
    )
```

```python
import functools

import jax
import jax.numpy as jnp
from jax import lax
from jax.experimental import pallas as pl
from jax.experimental.pallas import tpu as pltpu
from jax.sharding import PartitionSpec as P

GROUPS = 32
MESH = pl.DeviceIdType.MESH
T, S, NX, NZ = 64, 4, 4, 8
FR, ROWS, COLS, CH = 4, 8, 256, 128
BF, F32 = jnp.bfloat16, jnp.float32


def shifted(v):
    z = jnp.zeros((1, CH), v.dtype)
    left = jnp.concatenate([z, v[: COLS - 1]], axis=0)
    right = jnp.concatenate([v[1:], z], axis=0)
    return jnp.concatenate([left, v, right], axis=1)


def group_sum(x):
    lane = lax.broadcasted_iota(jnp.int32, x.shape, 1)
    n = x.shape[1]
    x = x + jnp.where(lane % 2 == 0, pltpu.roll(x, n - 1, 1), pltpu.roll(x, 1, 1))
    return x + jnp.where(lane % 4 < 2, pltpu.roll(x, n - 2, 1), pltpu.roll(x, 2, 1))


def conv_kernel(x, w, lens_hbm, acc, tab, lens, XL, XH, YU, YD, PA, W, sS, sQ, st, ct, buf1, buf2,
                lensem, tok, tok2, lsem, wsem, xsem_s, xsem_r, ysem_s, ysem_r, s1_s, s1_r, s2_s, s2_r):
    t = lax.axis_index("tm")
    y = lax.axis_index("space")
    core = t % 2
    chip = t // 2
    cx = chip % NX
    cz = chip // NX

    def dev(z_, x_, c_, y_):
        return ((z_ * NX + x_) * 2 + c_, y_)

    nxt = ((t + 1) % T, y)
    up = (t, (y + 1) % S)
    down = (t, (y + S - 1) % S)

    near = [(dc, dy) for dc in range(2) for dy in (2, 1, 3, 0) if (dc, dy) != (0, 0)]
    far = [(dz, dx) for dz in (2, -2, 1, -1, 0) for dx in (2, 1, 3, 0) if (dz, dx) != (0, 0)]

    def near_dev(dc, dy):
        return dev(cz, cx, (core + dc) % 2, (y + dy) % S)

    def far_dev(dz, dx):
        return dev((cz + dz + NZ) % NZ, (cx + dx) % NX, core, y)

    prev = ((t + T - 1) % T, y)
    direct = [nxt, up, down, prev, far_dev(0, 1), far_dev(0, 3), far_dev(1, 0), far_dev(-1, 0)]
    second = [far_dev(2, 0), far_dev(-2, 0), far_dev(1, 0), far_dev(-1, 0), near_dev(1, 0)]
    barrier = pltpu.get_barrier_semaphore()

    def greet(sem, devices):
        for d in devices:
            pl.semaphore_signal(sem, inc=1, device_id=d, device_id_type=MESH)

    greet(barrier, direct)
    lens_load = pltpu.make_async_copy(lens_hbm, lens, lensem)
    lens_load.start()
    loads = [pltpu.make_async_copy(x.at[f], XL.at[f], lsem.at[f]) for f in range(FR)]
    wloads = []
    for lag in range(3):
        wloads.append(pltpu.make_async_copy(w.at[lag], W.at[lag, pl.ds(0, 1152), pl.ds(0, 128)], wsem.at[lag]))
        wloads.append(pltpu.make_async_copy(w.at[lag], W.at[lag, pl.ds(384, 1152), pl.ds(128, 128)], wsem.at[3 + lag]))
    for c in loads + wloads:
        c.start()

    for lag in range(3):
        W[lag, 1152:1536, 0:128] = jnp.zeros((384, 128), BF)
        W[lag, 0:384, 128:256] = jnp.zeros((384, 128), BF)

    pl.semaphore_wait(barrier, len(direct))

    def rcopy(src, dst, ss, rs, d):
        return pltpu.make_async_remote_copy(src_ref=src, dst_ref=dst, send_sem=ss, recv_sem=rs, device_id=d, device_id_type=MESH)

    xc = []
    for i, (r0, n) in enumerate([(0, 1), (7, 1), (1, 2), (3, 2), (5, 2)]):
        xc.append(rcopy(x.at[pl.ds(2, 2), pl.ds(r0, n)], XH.at[:, pl.ds(r0, n)], xsem_s.at[i], xsem_r.at[i], nxt))
    yc = [
        rcopy(x.at[:, 7], YU.at[pl.ds(2, 4)], ysem_s.at[0], ysem_r.at[0], up),
        rcopy(x.at[:, 0], YD.at[pl.ds(2, 4)], ysem_s.at[1], ysem_r.at[1], down),
        rcopy(XH.at[:, 7], YU.at[pl.ds(0, 2)], ysem_s.at[2], ysem_r.at[2], up),
        rcopy(XH.at[:, 0], YD.at[pl.ds(0, 2)], ysem_s.at[3], ysem_r.at[3], down),
    ]
    xc[0].start()
    xc[1].start()
    yc[0].start()
    yc[1].start()
    xc[2].start()
    xc[3].start()
    xc[4].start()
    greet(tok, direct)

    lens_load.wait()
    pos = [t * FR + i for i in range(FR)]

    def bounds(k, c):
        cum, starts, ends = c
        after = cum + lens[k]
        inside = [(cum <= p) & (p < after) for p in pos]
        starts = tuple(jnp.where(i, cum, s) for i, s in zip(inside, starts))
        ends = tuple(jnp.where(i, after, e) for i, e in zip(inside, ends))
        return after, starts, ends

    zero = jnp.int32(0)
    _, starts, ends = lax.fori_loop(0, 32, bounds, (zero, (zero,) * FR, (zero,) * FR))
    within = [[jnp.where(pos[i] - lag >= starts[i], 1.0, 0.0).astype(F32) for lag in range(3)] for i in range(FR)]

    def build(f):
        for r in range(ROWS):
            e = r + 1
            PA[f + 2, e // 2, :, (e % 2) * 384 : (e % 2 + 1) * 384] = shifted(XL[f, r])

    def dot(a, b):
        return jnp.dot(a, b, preferred_element_type=F32)

    def unit(i, lag, first):
        a = PA[i + 2 - lag, 1:4].reshape(768, 768)
        d1 = dot(a, W[lag, 768:1536]).reshape(3, 256, 256)
        d0 = dot(a, W[lag, 0:768]).reshape(3, 256, 256)
        parts = [d1[0], d1[1] + d0[0], d1[2] + d0[1], d0[2]]
        for k in range(4):
            v = parts[k] if lag == 0 else within[i][lag] * parts[k]
            if first:
                acc[i, k] = v
            else:
                acc[i, k] += v

    for c in loads:
        c.wait()
    for c in wloads:
        c.wait()
    build(0)
    for f in range(FR):
        for lag in range(min(2, FR - 1 - f), -1, -1):
            unit(f + lag, lag, lag == min(2, f + lag))
        if f + 1 < FR:
            build(f + 1)
        if f == 1:
            pl.semaphore_wait(tok, len(direct))
            greet(tok2, second)
            xc[0].wait_recv()
            xc[1].wait_recv()
            yc[2].start()
            yc[3].start()

    has_up = y > 0
    has_down = y < S - 1
    yc[0].wait_recv()
    yc[1].wait_recv()
    zrow = jnp.zeros((COLS, CH), BF)

    def rims(f, _):
        PA[f, 0, :, 0:384] = shifted(jnp.where(has_up, YU[f], zrow))
        PA[f, 4, :, 384:768] = shifted(jnp.where(has_down, YD[f], zrow))
        return 0

    lax.fori_loop(2, 6, rims, 0)

    def rim_dots(lag, lo):
        n = FR - lo
        a = PA[lo + 2 - lag : FR + 2 - lag, 0].reshape(n * 256, 768)
        d = dot(a, W[lag, 0:768]).reshape(n, 256, 256)
        a2 = PA[lo + 2 - lag : FR + 2 - lag, 4].reshape(n * 256, 768)
        d2 = dot(a2, W[lag, 768:1536]).reshape(n, 256, 256)
        for i in range(lo, FR):
            acc[i, 0] += within[i][lag] * d[i - lo]
            acc[i, 3] += within[i][lag] * d2[i - lo]

    for lag in range(3):
        rim_dots(lag, lag)

    def stat(i, k):
        v = acc[i, k]
        s = jnp.sum(v, axis=0, keepdims=True)
        c = v - s * (1.0 / 256)
        q = jnp.sum(c * c, axis=0, keepdims=True)
        sS[i, pl.ds(k, 1)] = s
        sQ[i, pl.ds(k, 1)] = q

    def stat_loop(n, _):
        stat(2 + n // 4, n % 4)
        return 0

    lax.fori_loop(0, 8, stat_loop, 0)

    def early(p):
        a1 = PA[1, p]
        a2 = PA[0:2, p].reshape(512, 768)
        if p < 4:
            e = dot(a1, W[1, 0:768])
            g = dot(a2, W[2, 0:768])
            acc[0, p] += within[0][1] * e + within[0][2] * g[0:256]
            acc[1, p] += within[1][2] * g[256:512]
        if p > 0:
            e = dot(a1, W[1, 768:1536])
            g = dot(a2, W[2, 768:1536])
            acc[0, p - 1] += within[0][1] * e + within[0][2] * g[0:256]
            acc[1, p - 1] += within[1][2] * g[256:512]

    def early_rows(p):
        for f in range(2):
            PA[f, p, :, 0:384] = shifted(XH[f, 2 * p - 1])
            PA[f, p, :, 384:768] = shifted(XH[f, 2 * p])

    xc[2].wait_recv()
    early_rows(1)
    early(1)
    yc[2].wait_recv()
    yc[3].wait_recv()
    for f in range(2):
        PA[f, 0, :, 384:768] = shifted(XH[f, 0])
        PA[f, 4, :, 0:384] = shifted(XH[f, 7])
    lax.fori_loop(0, 2, rims, 0)
    early(0)
    early(4)
    stat(0, 0)
    stat(1, 0)
    xc[3].wait_recv()
    early_rows(2)
    early(2)
    stat(0, 1)
    stat(1, 1)
    xc[4].wait_recv()
    early_rows(3)
    early(3)
    stat(0, 2)
    stat(1, 2)
    stat(0, 3)
    stat(1, 3)

    means, squares = [], []
    for i in range(FR):
        s = sS[i]
        q = sQ[i]
        m = s * (1.0 / 256)
        tot = jnp.sum(s, axis=0, keepdims=True)
        mean = (tot[:, :128] + tot[:, 128:]) * (1.0 / 2048)
        both = jnp.concatenate([mean, mean], axis=1)
        dm = m - both
        qq = jnp.sum(q + 256.0 * dm * dm, axis=0, keepdims=True)
        means.append(mean)
        squares.append(qq[:, :128] + qq[:, 128:])
    mine = jnp.concatenate(means + squares, axis=0)
    st[...] = mine
    buf1[core * S + y] = mine

    s1 = []
    for i, (dc, dy) in enumerate(near):
        s1.append(rcopy(st, buf1.at[core * S + y], s1_s.at[i], s1_r.at[i], near_dev(dc, dy)))
    pl.semaphore_wait(tok2, len(second))
    for c in s1:
        c.start()
    for c in xc + yc:
        c.wait_send()
    for c in s1:
        c.wait_recv()

    parts = []
    for c in range(2):
        b = buf1[pl.ds(c * S, S)]
        m = b[:, 0:4]
        mean = jnp.sum(m, axis=0) * (1.0 / S)
        dm = m - mean[None]
        parts.append((mean, jnp.sum(b[:, 4:8] + 2048.0 * dm * dm, axis=0)))
    chip_table = jnp.concatenate([parts[0][0], parts[1][0], parts[0][1], parts[1][1]], axis=0)
    ct[...] = chip_table
    buf2[2 * NX + cx] = chip_table

    s2 = []
    for i, (dz, dx) in enumerate(far):
        s2.append(rcopy(ct, buf2.at[(2 - dz) * NX + cx], s2_s.at[i], s2_r.at[i], far_dev(dz, dx)))
    for c in s2:
        c.start()
    for c in s1:
        c.wait_send()
    weight = [1.0 / (jnp.full((1, 128), 4.0, F32) * (ends[i] - starts[i]).astype(F32)) for i in range(FR)]
    for c in s2:
        c.wait_recv()

    shape = (5 * NX, 8, 128)
    slot = lax.broadcasted_iota(jnp.int32, shape, 0)
    row = lax.broadcasted_iota(jnp.int32, shape, 1)
    frame = ((cz - 2) * NX + slot) * 8 + row
    mean_e = buf2[:, 0:8]
    m2_e = buf2[:, 8:16]
    masks = [((frame >= starts[i]) & (frame < ends[i])).astype(F32) for i in range(FR)]
    total = [jnp.sum(jnp.sum(masks[i] * mean_e, axis=0), axis=0, keepdims=True) * weight[i] for i in range(FR)]
    avg = group_sum(jnp.concatenate(total + total, axis=0))
    vs = []
    for i in range(FR):
        d = mean_e - avg[i : i + 1][None]
        e = masks[i] * (m2_e + 8192.0 * d * d)
        vs.append(jnp.sum(jnp.sum(e, axis=0), axis=0, keepdims=True) * (weight[i] * (1.0 / 8192)))
    var = group_sum(jnp.concatenate(vs + vs, axis=0))
    rstd = lax.rsqrt(var + 1e-6)
    tab[...] = jnp.concatenate([avg[0:4], rstd[0:4]], axis=0)

    for c in s2:
        c.wait_send()


def norm_kernel(acc, tab, gain, shift, out, buf, sem):
    off = shift[...] * 0.5
    copies = []
    for c in range(8):
        i, p = c // 2, 2 * (c % 2)
        avg = tab[i : i + 1]
        scale = tab[i + 4 : i + 5] * gain[...] * 0.5
        for k in (p, p + 1):
            for h in range(2):
                v = (acc[i, k, :, h * 128 : (h + 1) * 128] - avg) * scale + off
                buf[i, 2 * k + h] = (v + v * jnp.tanh(v)).astype(BF)
        copies.append(pltpu.make_async_copy(buf.at[i, pl.ds(2 * p, 4)], out.at[i, pl.ds(2 * p, 4)], sem.at[c]))
        copies[-1].start()
    for c in copies:
        c.wait()


def shards(frames, conv_weight, norm_gain, norm_shift, clip_lengths):
    V = pltpu.VMEM

    def hbm(a):
        return pltpu.with_memory_space_constraint(a, pltpu.HBM)

    D = pltpu.SemaphoreType.DMA
    anyspec = pl.BlockSpec(memory_space=pltpu.HBM)
    vspec = pl.BlockSpec(memory_space=V)
    acc, tab = pl.pallas_call(
        conv_kernel,
        out_shape=(pltpu.VMEM((FR, 4, 256, 256), F32), pltpu.VMEM((8, 128), F32)),
        in_specs=[anyspec, anyspec, anyspec],
        out_specs=(vspec, vspec),
        scratch_shapes=[
            pltpu.SMEM((32,), jnp.int32),
            V((4, 8, 256, 128), BF), V((2, 8, 256, 128), BF), V((6, 256, 128), BF), V((6, 256, 128), BF),
            V((6, 5, 256, 768), BF), V((3, 1536, 256), BF),
            V((4, 4, 256), F32), V((4, 4, 256), F32), V((8, 128), F32), V((16, 128), F32),
            V((8, 8, 128), F32), V((20, 16, 128), F32),
            D, pltpu.SemaphoreType.REGULAR, pltpu.SemaphoreType.REGULAR,
            D((4,)), D((6,)), D((5,)), D((5,)), D((4,)), D((4,)), D((7,)), D((7,)), D((19,)), D((19,)),
        ],
        compiler_params=pltpu.CompilerParams(collective_id=0, has_side_effects=True, vmem_limit_bytes=56 * 2**20),
        name="conv_stats",
    )(hbm(frames), hbm(conv_weight), hbm(clip_lengths))
    return pl.pallas_call(
        norm_kernel,
        out_shape=jax.ShapeDtypeStruct((FR, ROWS, COLS, CH), BF),
        in_specs=[vspec, vspec, vspec, vspec],
        out_specs=anyspec,
        scratch_shapes=[V((FR, ROWS, COLS, CH), BF), D((8,))],
        compiler_params=pltpu.CompilerParams(vmem_limit_bytes=8 * 2**20),
        name="normalize",
    )(
        pltpu.with_memory_space_constraint(acc, V),
        pltpu.with_memory_space_constraint(tab, V),
        norm_gain.reshape(1, CH),
        norm_shift.reshape(1, CH),
    )


def solution(mesh):
    return jax.shard_map(
        shards,
        mesh=mesh,
        in_specs=(P("tm", "space", None, None), P(), P(), P(), P()),
        out_specs=P("tm", "space", None, None),
        check_vma=False,
    )
```

```python
import functools

import jax
import jax.numpy as jnp
from jax import lax
from jax.experimental import pallas as pl
from jax.experimental.pallas import tpu as pltpu
from jax.sharding import PartitionSpec as P

GROUPS = 32
MESH = pl.DeviceIdType.MESH
T, S, NX, NZ = 64, 4, 4, 8
FR, ROWS, COLS, CH = 4, 8, 256, 128
BF, F32 = jnp.bfloat16, jnp.float32


def shifted(v):
    z = jnp.zeros((1, CH), v.dtype)
    left = jnp.concatenate([z, v[: COLS - 1]], axis=0)
    right = jnp.concatenate([v[1:], z], axis=0)
    return jnp.concatenate([left, v, right], axis=1)


def group_sum(x):
    lane = lax.broadcasted_iota(jnp.int32, x.shape, 1)
    n = x.shape[1]
    x = x + jnp.where(lane % 2 == 0, pltpu.roll(x, n - 1, 1), pltpu.roll(x, 1, 1))
    return x + jnp.where(lane % 4 < 2, pltpu.roll(x, n - 2, 1), pltpu.roll(x, 2, 1))


def conv_kernel(x, w, lens_hbm, acc, tab, lens, XL, XH, YU, YD, PA, W, sS, sQ, st, ct, buf1, buf2,
                lensem, tok, tok2, lsem, wsem, xsem_s, xsem_r, ysem_s, ysem_r, s1_s, s1_r, s2_s, s2_r):
    t = lax.axis_index("tm")
    y = lax.axis_index("space")
    core = t % 2
    chip = t // 2
    cx = chip % NX
    cz = chip // NX

    def dev(z_, x_, c_, y_):
        return ((z_ * NX + x_) * 2 + c_, y_)

    nxt = ((t + 1) % T, y)
    up = (t, (y + 1) % S)
    down = (t, (y + S - 1) % S)

    near = [(dc, dy) for dc in range(2) for dy in (2, 1, 3, 0) if (dc, dy) != (0, 0)]
    far = [(dz, dx) for dz in (2, -2, 1, -1, 0) for dx in (2, 1, 3, 0) if (dz, dx) != (0, 0)]

    def near_dev(dc, dy):
        return dev(cz, cx, (core + dc) % 2, (y + dy) % S)

    def far_dev(dz, dx):
        return dev((cz + dz + NZ) % NZ, (cx + dx) % NX, core, y)

    has_next = t < T - 1
    has_prev = t > 0

    def has_z(dz):
        return (cz + dz >= 0) & (cz + dz < NZ)

    prev = ((t + T - 1) % T, y)
    direct = [(nxt, has_next), (up, None), (down, None), (prev, has_prev), (far_dev(0, 1), None), (far_dev(0, 3), None),
              (far_dev(1, 0), has_z(1)), (far_dev(-1, 0), has_z(-1))]
    second = [(far_dev(2, 0), has_z(2)), (far_dev(-2, 0), has_z(-2)), (far_dev(1, 0), has_z(1)), (far_dev(-1, 0), has_z(-1)),
              (near_dev(1, 0), None)]
    barrier = pltpu.get_barrier_semaphore()

    def greet(sem, devices):
        for d, cond in devices:
            def signal(d=d):
                pl.semaphore_signal(sem, inc=1, device_id=d, device_id_type=MESH)
            if cond is None:
                signal()
            else:
                pl.when(cond)(signal)

    def count(devices):
        return sum(jnp.int32(1) if cond is None else cond.astype(jnp.int32) for _, cond in devices)

    buf2[...] = jnp.zeros_like(buf2)
    greet(barrier, direct)
    lens_load = pltpu.make_async_copy(lens_hbm, lens, lensem)
    lens_load.start()
    loads = [pltpu.make_async_copy(x.at[f], XL.at[f], lsem.at[f]) for f in range(FR)]
    wloads = [pltpu.make_async_copy(w.at[lag], W.at[lag, pl.ds(0, 1152), pl.ds(0, 128)], wsem.at[lag]) for lag in range(3)]
    for c in [loads[0]] + wloads + loads[1:]:
        c.start()

    for lag in range(3):
        W[lag, 1152:1536, 0:128] = jnp.zeros((384, 128), BF)
        W[lag, 0:384, 128:256] = jnp.zeros((384, 128), BF)

    pl.semaphore_wait(barrier, count(direct))

    def rcopy(src, dst, ss, rs, d):
        return pltpu.make_async_remote_copy(src_ref=src, dst_ref=dst, send_sem=ss, recv_sem=rs, device_id=d, device_id_type=MESH)

    xc = []
    for i, (r0, n) in enumerate([(0, 1), (7, 1), (1, 2), (3, 2), (5, 2)]):
        xc.append(rcopy(x.at[pl.ds(2, 2), pl.ds(r0, n)], XH.at[:, pl.ds(r0, n)], xsem_s.at[i], xsem_r.at[i], nxt))
    yc = [
        rcopy(x.at[:, 7], YU.at[pl.ds(2, 4)], ysem_s.at[0], ysem_r.at[0], up),
        rcopy(x.at[:, 0], YD.at[pl.ds(2, 4)], ysem_s.at[1], ysem_r.at[1], down),
        rcopy(XH.at[:, 7], YU.at[pl.ds(0, 2)], ysem_s.at[2], ysem_r.at[2], up),
        rcopy(XH.at[:, 0], YD.at[pl.ds(0, 2)], ysem_s.at[3], ysem_r.at[3], down),
    ]
    @pl.when(has_next)
    def _():
        xc[0].start()
        xc[1].start()

    yc[0].start()
    yc[1].start()

    @pl.when(has_next)
    def _():
        for c in xc[2:]:
            c.start()

    @pl.when(jnp.logical_not(has_prev))
    def _():
        XH[...] = jnp.zeros_like(XH)

    def landed(*copies):
        @pl.when(has_prev)
        def _():
            for c in copies:
                c.wait_recv()

    greet(tok, direct)

    lens_load.wait()
    pos = [t * FR + i for i in range(FR)]

    def bounds(k, c):
        cum, starts, ends = c
        after = cum + lens[k]
        inside = [(cum <= p) & (p < after) for p in pos]
        starts = tuple(jnp.where(i, cum, s) for i, s in zip(inside, starts))
        ends = tuple(jnp.where(i, after, e) for i, e in zip(inside, ends))
        return after, starts, ends

    zero = jnp.int32(0)
    _, starts, ends = lax.fori_loop(0, 32, bounds, (zero, (zero,) * FR, (zero,) * FR))
    within = [[jnp.where(pos[i] - lag >= starts[i], 1.0, 0.0).astype(F32) for lag in range(3)] for i in range(FR)]

    def build(f):
        for r in range(ROWS):
            e = r + 1
            PA[f + 2, e // 2, :, (e % 2) * 384 : (e % 2 + 1) * 384] = shifted(XL[f, r])

    def dot(a, b):
        return jnp.dot(a, b, preferred_element_type=F32)

    for c in loads:
        c.wait()
    build(0)
    for lag in range(3):
        wloads[lag].wait()
        W[lag, 384:1536, 128:256] = W[lag, 0:1152, 0:128]
    for f in range(FR):
        tot = None
        for lag in range(min(f, 2), -1, -1):
            a = PA[f + 2 - lag, 1:4].reshape(768, 768)
            d1 = dot(a, W[lag, 768:1536])
            d0 = dot(a, W[lag, 0:768])
            if lag:
                d1 = d1 * within[f][lag]
                d0 = d0 * within[f][lag]
            tot = (d1, d0) if tot is None else (tot[0] + d1, tot[1] + d0)
        d1, d0 = tot[0].reshape(3, 256, 256), tot[1].reshape(3, 256, 256)
        acc[f, 0] = d1[0]
        acc[f, 1] = d1[1] + d0[0]
        acc[f, 2] = d1[2] + d0[1]
        acc[f, 3] = d0[2]
        if f + 1 < FR:
            build(f + 1)
        if f == 1:
            pl.semaphore_wait(tok, count(direct))
            greet(tok2, second)
            landed(xc[0], xc[1])
            yc[2].start()
            yc[3].start()

    def stat(i, k):
        v = acc[i, k]
        s = jnp.sum(v, axis=0, keepdims=True)
        c = v - s * (1.0 / 256)
        q = jnp.sum(c * c, axis=0, keepdims=True)
        sS[i, k : k + 1] = s
        sQ[i, k : k + 1] = q

    has_up = y > 0
    has_down = y < S - 1
    yc[0].wait_recv()
    yc[1].wait_recv()
    zrow = jnp.zeros((COLS, CH), BF)

    def rims(f, _):
        PA[f, 0, :, 0:384] = shifted(jnp.where(has_up, YU[f], zrow))
        PA[f, 4, :, 384:768] = shifted(jnp.where(has_down, YD[f], zrow))
        return 0

    for f in range(2, 6):
        rims(f, 0)

    def rim_dots(lag, lo):
        n = FR - lo
        a = PA[lo + 2 - lag : FR + 2 - lag, 0].reshape(n * 256, 768)
        d = dot(a, W[lag, 0:768]).reshape(n, 256, 256)
        a2 = PA[lo + 2 - lag : FR + 2 - lag, 4].reshape(n * 256, 768)
        d2 = dot(a2, W[lag, 768:1536]).reshape(n, 256, 256)
        for i in range(lo, FR):
            acc[i, 0] += within[i][lag] * d[i - lo]
            acc[i, 3] += within[i][lag] * d2[i - lo]

    for lag in range(3):
        rim_dots(lag, lag)
    for i, k in ((2, 1), (2, 2), (3, 1), (3, 2)):
        stat(i, k)

    def early(p):
        a1 = PA[1, p]
        a2 = PA[0:2, p].reshape(512, 768)
        if p < 4:
            e = dot(a1, W[1, 0:768])
            g = dot(a2, W[2, 0:768])
            acc[0, p] += within[0][1] * e + within[0][2] * g[0:256]
            acc[1, p] += within[1][2] * g[256:512]
        if p > 0:
            e = dot(a1, W[1, 768:1536])
            g = dot(a2, W[2, 768:1536])
            acc[0, p - 1] += within[0][1] * e + within[0][2] * g[0:256]
            acc[1, p - 1] += within[1][2] * g[256:512]

    def early_rows(p):
        for f in range(2):
            PA[f, p, :, 0:384] = shifted(XH[f, 2 * p - 1])
            PA[f, p, :, 384:768] = shifted(XH[f, 2 * p])

    landed(xc[2])
    early_rows(1)
    early(1)
    for i, k in ((2, 0), (2, 3), (3, 0), (3, 3)):
        stat(i, k)
    yc[2].wait_recv()
    yc[3].wait_recv()
    for f in range(2):
        PA[f, 0, :, 384:768] = shifted(XH[f, 0])
        PA[f, 4, :, 0:384] = shifted(XH[f, 7])
    for f in range(2):
        rims(f, 0)
    early(0)
    early(4)
    landed(xc[3])
    early_rows(2)
    early(2)
    stat(0, 0)
    stat(1, 0)
    landed(xc[4])
    early_rows(3)
    early(3)
    for i, k in ((0, 1), (1, 1), (0, 2), (1, 2), (0, 3), (1, 3)):
        stat(i, k)

    lane = lax.broadcasted_iota(jnp.int32, (FR, 128), 1) % 4
    means, squares = [], []
    for i in range(FR):
        s = sS[i]
        m = s * (1.0 / 256)
        tot = jnp.sum(s, axis=0, keepdims=True)
        mean = (tot[:, :128] + tot[:, 128:]) * (1.0 / 2048)
        dm = m - jnp.concatenate([mean, mean], axis=1)
        qq = jnp.sum(sQ[i] + 256.0 * dm * dm, axis=0, keepdims=True)
        means.append(mean)
        squares.append(qq[:, :128] + qq[:, 128:])
    m = jnp.concatenate(means, axis=0)
    g = group_sum(m) * 0.25
    dm = m - g
    mine = jnp.where(lane == 0, g, group_sum(jnp.concatenate(squares, axis=0) + 2048.0 * dm * dm))
    st[...] = mine
    buf1[core * S + y] = mine

    s1 = []
    for i, (dc, dy) in enumerate(near):
        s1.append(rcopy(st, buf1.at[core * S + y], s1_s.at[i], s1_r.at[i], near_dev(dc, dy)))
    pl.semaphore_wait(tok2, count(second))
    for c in s1:
        c.start()

    @pl.when(has_next)
    def _():
        for c in xc:
            c.wait_send()

    for c in yc:
        c.wait_send()
    weight = [1.0 / (jnp.full((1, 128), 1.0, F32) * (ends[i] - starts[i]).astype(F32)) for i in range(FR)]
    for c in s1:
        c.wait_recv()

    parts = []
    for c in range(2):
        b = buf1[pl.ds(c * S, S)]
        tot = jnp.sum(b, axis=0)
        mean = tot * (1.0 / S)
        dm = b - mean[None]
        parts.append(jnp.where(lane == 0, mean, tot + 8192.0 * pltpu.roll(jnp.sum(dm * dm, axis=0), 1, 1)))
    chip_table = jnp.concatenate(parts, axis=0)
    ct[...] = chip_table
    buf2[2 * NX + cx] = chip_table

    s2 = {}
    for i, (dz, dx) in enumerate(far):
        c = rcopy(ct, buf2.at[(2 - dz) * NX + cx], s2_s.at[i], s2_r.at[i], far_dev(dz, dx))
        s2.setdefault(dz, []).append(c)

    def each(dz, there, act):
        def run():
            for c in s2[dz]:
                act(c)
        pl.when(has_z(there))(run)

    for dz in s2:
        each(dz, dz, lambda c: c.start())
    for c in s1:
        c.wait_send()
    for dz in s2:
        each(dz, -dz, lambda c: c.wait_recv())

    shape = (5 * NX, 8, 128)
    frame = ((cz - 2) * NX + lax.broadcasted_iota(jnp.int32, shape, 0)) * 8 + lax.broadcasted_iota(jnp.int32, shape, 1)
    entry = buf2[...]
    avgs, vs = [], []
    for i in range(FR):
        mask = ((frame >= starts[i]) & (frame < ends[i])).astype(F32)
        tot = jnp.sum(jnp.sum(mask * entry, axis=0), axis=0, keepdims=True) * weight[i]
        d = entry - tot[None]
        dd = jnp.sum(jnp.sum(mask * (d * d), axis=0), axis=0, keepdims=True) * weight[i]
        avgs.append(tot)
        vs.append(tot * (1.0 / 32768) + pltpu.roll(dd, 1, 1))
    both = jnp.concatenate(avgs + vs, axis=0)
    lane8 = lax.broadcasted_iota(jnp.int32, (8, 128), 1) % 4
    row8 = lax.broadcasted_iota(jnp.int32, (8, 128), 0)
    both = group_sum(jnp.where(lane8 == jnp.where(row8 < 4, 0, 1), both, 0.0))
    tab[...] = jnp.where(row8 < 4, both, lax.rsqrt(both + 1e-6))

    for dz in s2:
        each(dz, dz, lambda c: c.wait_send())


def norm_kernel(acc, tab, gain, shift, out, buf, sem):
    off = shift[...] * 0.5
    copies = []
    for c in range(8):
        i, p = c // 2, 2 * (c % 2)
        avg = tab[i : i + 1]
        scale = tab[i + 4 : i + 5] * gain[...] * 0.5
        for k in (p, p + 1):
            for h in range(2):
                v = (acc[i, k, :, h * 128 : (h + 1) * 128] - avg) * scale + off
                buf[i, 2 * k + h] = (v + v * jnp.tanh(v)).astype(BF)
        copies.append(pltpu.make_async_copy(buf.at[i, pl.ds(2 * p, 4)], out.at[i, pl.ds(2 * p, 4)], sem.at[c]))
        copies[-1].start()
    for c in copies:
        c.wait()


def shards(frames, conv_weight, norm_gain, norm_shift, clip_lengths):
    V = pltpu.VMEM

    def hbm(a):
        return pltpu.with_memory_space_constraint(a, pltpu.HBM)

    D = pltpu.SemaphoreType.DMA
    anyspec = pl.BlockSpec(memory_space=pltpu.HBM)
    vspec = pl.BlockSpec(memory_space=V)
    acc, tab = pl.pallas_call(
        conv_kernel,
        out_shape=(pltpu.VMEM((FR, 4, 256, 256), F32), pltpu.VMEM((8, 128), F32)),
        in_specs=[anyspec, anyspec, anyspec],
        out_specs=(vspec, vspec),
        scratch_shapes=[
            pltpu.SMEM((32,), jnp.int32),
            V((4, 8, 256, 128), BF), V((2, 8, 256, 128), BF), V((6, 256, 128), BF), V((6, 256, 128), BF),
            V((6, 5, 256, 768), BF), V((3, 1536, 256), BF),
            V((4, 4, 256), F32), V((4, 4, 256), F32), V((4, 128), F32), V((8, 128), F32),
            V((8, 4, 128), F32), V((20, 8, 128), F32),
            D, pltpu.SemaphoreType.REGULAR, pltpu.SemaphoreType.REGULAR,
            D((4,)), D((3,)), D((5,)), D((5,)), D((4,)), D((4,)), D((7,)), D((7,)), D((19,)), D((19,)),
        ],
        compiler_params=pltpu.CompilerParams(collective_id=0, has_side_effects=True, vmem_limit_bytes=56 * 2**20),
        name="conv_stats",
    )(hbm(frames), hbm(conv_weight), hbm(clip_lengths))
    return pl.pallas_call(
        norm_kernel,
        out_shape=jax.ShapeDtypeStruct((FR, ROWS, COLS, CH), BF),
        in_specs=[vspec, vspec, vspec, vspec],
        out_specs=anyspec,
        scratch_shapes=[V((FR, ROWS, COLS, CH), BF), D((8,))],
        compiler_params=pltpu.CompilerParams(vmem_limit_bytes=8 * 2**20),
        name="normalize",
    )(
        pltpu.with_memory_space_constraint(acc, V),
        pltpu.with_memory_space_constraint(tab, V),
        norm_gain.reshape(1, CH),
        norm_shift.reshape(1, CH),
    )


def solution(mesh):
    return jax.shard_map(
        shards,
        mesh=mesh,
        in_specs=(P("tm", "space", None, None), P(), P(), P(), P()),
        out_specs=P("tm", "space", None, None),
        check_vma=False,
    )
```

```python
import functools

import jax
import jax.numpy as jnp
from jax import lax
from jax.experimental import pallas as pl
from jax.experimental.pallas import tpu as pltpu
from jax.sharding import PartitionSpec as P

GROUPS = 32
MESH = pl.DeviceIdType.MESH
T, S, NX, NZ = 64, 4, 4, 8
FR, ROWS, COLS, CH = 4, 8, 256, 128
BF, F32 = jnp.bfloat16, jnp.float32


def shifted(v):
    z = jnp.zeros((1, CH), v.dtype)
    left = jnp.concatenate([z, v[: COLS - 1]], axis=0)
    right = jnp.concatenate([v[1:], z], axis=0)
    return jnp.concatenate([left, v, right], axis=1)


def group_sum(x):
    lane = lax.broadcasted_iota(jnp.int32, x.shape, 1)
    n = x.shape[1]
    x = x + jnp.where(lane % 2 == 0, pltpu.roll(x, n - 1, 1), pltpu.roll(x, 1, 1))
    return x + jnp.where(lane % 4 < 2, pltpu.roll(x, n - 2, 1), pltpu.roll(x, 2, 1))


def conv_kernel(x, w, lens_hbm, acc, tab, lens, XL, XH, YU, YD, PA, W, sS, sQ, st, ct, buf1, buf2,
                lensem, tok, tok2, lsem, wsem, xsem_s, xsem_r, ysem_s, ysem_r, s1_s, s1_r, s2_s, s2_r):
    t = lax.axis_index("tm")
    y = lax.axis_index("space")
    core = t % 2
    chip = t // 2
    cx = chip % NX
    cz = chip // NX

    def dev(z_, x_, c_, y_):
        return ((z_ * NX + x_) * 2 + c_, y_)

    nxt = ((t + 1) % T, y)
    up = (t, (y + 1) % S)
    down = (t, (y + S - 1) % S)

    near = [(dc, dy) for dc in range(2) for dy in (2, 1, 3, 0) if (dc, dy) != (0, 0)]
    far = [(dz, dx) for dz in (2, -2, 1, -1, 0) for dx in (2, 1, 3, 0) if (dz, dx) != (0, 0)]

    def near_dev(dc, dy):
        return dev(cz, cx, (core + dc) % 2, (y + dy) % S)

    def far_dev(dz, dx):
        return dev((cz + dz + NZ) % NZ, (cx + dx) % NX, core, y)

    has_next = t < T - 1
    has_prev = t > 0

    def has_z(dz):
        return (cz + dz >= 0) & (cz + dz < NZ)

    prev = ((t + T - 1) % T, y)
    direct = [(nxt, has_next), (up, None), (down, None), (prev, has_prev), (far_dev(0, 1), None), (far_dev(0, 3), None),
              (far_dev(1, 0), has_z(1)), (far_dev(-1, 0), has_z(-1))]
    second = [(far_dev(2, 0), has_z(2)), (far_dev(-2, 0), has_z(-2)), (far_dev(1, 0), has_z(1)), (far_dev(-1, 0), has_z(-1)),
              (near_dev(1, 0), None)]
    barrier = pltpu.get_barrier_semaphore()

    def greet(sem, devices):
        for d, cond in devices:
            def signal(d=d):
                pl.semaphore_signal(sem, inc=1, device_id=d, device_id_type=MESH)
            if cond is None:
                signal()
            else:
                pl.when(cond)(signal)

    def count(devices):
        return sum(jnp.int32(1) if cond is None else cond.astype(jnp.int32) for _, cond in devices)

    buf2[...] = jnp.zeros_like(buf2)
    greet(barrier, direct)
    lens_load = pltpu.make_async_copy(lens_hbm, lens, lensem)
    lens_load.start()
    loads = [pltpu.make_async_copy(x.at[f], XL.at[f], lsem.at[f]) for f in range(FR)]
    wloads = [pltpu.make_async_copy(w.at[lag], W.at[lag, pl.ds(0, 1152), pl.ds(0, 128)], wsem.at[lag]) for lag in range(3)]
    for c in (loads[0], wloads[0], loads[1], wloads[1], loads[2], wloads[2], loads[3]):
        c.start()

    for lag in range(3):
        W[lag, 1152:1536, 0:128] = jnp.zeros((384, 128), BF)
        W[lag, 0:384, 128:256] = jnp.zeros((384, 128), BF)

    pl.semaphore_wait(barrier, count(direct))

    def rcopy(src, dst, ss, rs, d):
        return pltpu.make_async_remote_copy(src_ref=src, dst_ref=dst, send_sem=ss, recv_sem=rs, device_id=d, device_id_type=MESH)

    xc = []
    for i, (r0, n) in enumerate([(0, 1), (7, 1), (1, 2), (3, 2), (5, 2)]):
        xc.append(rcopy(x.at[pl.ds(2, 2), pl.ds(r0, n)], XH.at[:, pl.ds(r0, n)], xsem_s, xsem_r.at[i], nxt))
    yc = [
        rcopy(x.at[:, 7], YU.at[pl.ds(2, 4)], ysem_s, ysem_r.at[0], up),
        rcopy(x.at[:, 0], YD.at[pl.ds(2, 4)], ysem_s, ysem_r.at[1], down),
        rcopy(XH.at[:, 7], YU.at[pl.ds(0, 2)], ysem_s, ysem_r.at[2], up),
        rcopy(XH.at[:, 0], YD.at[pl.ds(0, 2)], ysem_s, ysem_r.at[3], down),
    ]
    @pl.when(has_next)
    def _():
        xc[0].start()
        xc[1].start()

    yc[0].start()
    yc[1].start()

    @pl.when(has_next)
    def _():
        for c in xc[2:]:
            c.start()

    @pl.when(jnp.logical_not(has_prev))
    def _():
        XH[...] = jnp.zeros_like(XH)

    def landed(*copies):
        @pl.when(has_prev)
        def _():
            for c in copies:
                c.wait_recv()


    lens_load.wait()
    pos = [t * FR + i for i in range(FR)]

    def bounds(k, c):
        cum, starts, ends = c
        after = cum + lens[k]
        inside = [(cum <= p) & (p < after) for p in pos]
        starts = tuple(jnp.where(i, cum, s) for i, s in zip(inside, starts))
        ends = tuple(jnp.where(i, after, e) for i, e in zip(inside, ends))
        return after, starts, ends

    zero = jnp.int32(0)
    _, starts, ends = lax.fori_loop(0, 32, bounds, (zero, (zero,) * FR, (zero,) * FR))
    within = [[jnp.where(pos[i] - lag >= starts[i], 1.0, 0.0).astype(F32) for lag in range(3)] for i in range(FR)]

    def build(f):
        for r in range(ROWS):
            e = r + 1
            PA[f + 2, e // 2, :, (e % 2) * 384 : (e % 2 + 1) * 384] = shifted(XL[f, r])

    def dot(a, b):
        return jnp.dot(a, b, preferred_element_type=F32)

    loads[0].wait()
    build(0)
    for f in range(FR):
        if f + 1 < FR:
            loads[f + 1].wait()
        if f < 3:
            wloads[f].wait()
            W[f, 384:1536, 128:256] = W[f, 0:1152, 0:128]
        tot = None
        for lag in range(min(f, 2), -1, -1):
            a = PA[f + 2 - lag, 1:4].reshape(768, 768)
            d1 = dot(a, W[lag, 768:1536])
            d0 = dot(a, W[lag, 0:768])
            if lag:
                d1 = d1 * within[f][lag]
                d0 = d0 * within[f][lag]
            tot = (d1, d0) if tot is None else (tot[0] + d1, tot[1] + d0)
        d1, d0 = tot[0].reshape(3, 256, 256), tot[1].reshape(3, 256, 256)
        acc[f, 0] = d1[0]
        acc[f, 1] = d1[1] + d0[0]
        acc[f, 2] = d1[2] + d0[1]
        acc[f, 3] = d0[2]
        if f + 1 < FR:
            build(f + 1)
        if f == 0:
            greet(tok, direct)
        if f == 2:
            landed(xc[0], xc[1])
            yc[2].start()
            yc[3].start()
            pl.semaphore_wait(tok, count(direct))
            greet(tok2, second)

    def stat(i, k):
        v = acc[i, k]
        s = jnp.sum(v, axis=0, keepdims=True)
        c = v - s * (1.0 / 256)
        q = jnp.sum(c * c, axis=0, keepdims=True)
        sS[i, k : k + 1] = s
        sQ[i, k : k + 1] = q

    has_up = y > 0
    has_down = y < S - 1
    yc[0].wait_recv()
    yc[1].wait_recv()
    zrow = jnp.zeros((COLS, CH), BF)

    def rims(f, _):
        PA[f, 0, :, 0:384] = shifted(jnp.where(has_up, YU[f], zrow))
        PA[f, 4, :, 384:768] = shifted(jnp.where(has_down, YD[f], zrow))
        return 0

    for f in range(2, 6):
        rims(f, 0)

    def rim_dots(lag, lo):
        n = FR - lo
        a = PA[lo + 2 - lag : FR + 2 - lag, 0].reshape(n * 256, 768)
        d = dot(a, W[lag, 0:768]).reshape(n, 256, 256)
        a2 = PA[lo + 2 - lag : FR + 2 - lag, 4].reshape(n * 256, 768)
        d2 = dot(a2, W[lag, 768:1536]).reshape(n, 256, 256)
        for i in range(lo, FR):
            acc[i, 0] += within[i][lag] * d[i - lo]
            acc[i, 3] += within[i][lag] * d2[i - lo]

    for lag in range(3):
        rim_dots(lag, lag)
    for i, k in ((2, 1), (2, 2), (3, 1), (3, 2)):
        stat(i, k)

    def early(p):
        a1 = PA[1, p]
        a2 = PA[0:2, p].reshape(512, 768)
        if p < 4:
            e = dot(a1, W[1, 0:768])
            g = dot(a2, W[2, 0:768])
            acc[0, p] += within[0][1] * e + within[0][2] * g[0:256]
            acc[1, p] += within[1][2] * g[256:512]
        if p > 0:
            e = dot(a1, W[1, 768:1536])
            g = dot(a2, W[2, 768:1536])
            acc[0, p - 1] += within[0][1] * e + within[0][2] * g[0:256]
            acc[1, p - 1] += within[1][2] * g[256:512]

    def early_rows(p):
        for f in range(2):
            PA[f, p, :, 0:384] = shifted(XH[f, 2 * p - 1])
            PA[f, p, :, 384:768] = shifted(XH[f, 2 * p])

    landed(xc[2])
    early_rows(1)
    early(1)
    for i, k in ((2, 0), (2, 3), (3, 0), (3, 3)):
        stat(i, k)
    yc[2].wait_recv()
    yc[3].wait_recv()
    for f in range(2):
        PA[f, 0, :, 384:768] = shifted(XH[f, 0])
        PA[f, 4, :, 0:384] = shifted(XH[f, 7])
    for f in range(2):
        rims(f, 0)
    early(0)
    early(4)
    landed(xc[3])
    early_rows(2)
    early(2)
    stat(0, 0)
    stat(1, 0)
    landed(xc[4])
    early_rows(3)
    early(3)
    for i, k in ((0, 1), (1, 1), (0, 2), (1, 2), (0, 3), (1, 3)):
        stat(i, k)

    lane = lax.broadcasted_iota(jnp.int32, (FR, 128), 1) % 4
    means, squares = [], []
    for i in range(FR):
        s = sS[i]
        m = s * (1.0 / 256)
        tot = jnp.sum(s, axis=0, keepdims=True)
        mean = (tot[:, :128] + tot[:, 128:]) * (1.0 / 2048)
        dm = m - jnp.concatenate([mean, mean], axis=1)
        qq = jnp.sum(sQ[i] + 256.0 * dm * dm, axis=0, keepdims=True)
        means.append(mean)
        squares.append(qq[:, :128] + qq[:, 128:])
    m = jnp.concatenate(means, axis=0)
    g = group_sum(m) * 0.25
    dm = m - g
    mine = jnp.where(lane == 0, g, group_sum(jnp.concatenate(squares, axis=0) + 2048.0 * dm * dm))
    st[...] = mine
    buf1[core * S + y] = mine

    s1 = []
    for dc, dy in near:
        s1.append(rcopy(st, buf1.at[core * S + y], s1_s, s1_r, near_dev(dc, dy)))
    pl.semaphore_wait(tok2, count(second))
    for c in s1:
        c.start()

    @pl.when(has_next)
    def _():
        rcopy(XH, XH, xsem_s, xsem_r.at[0], nxt).wait_send()

    rcopy(x.at[:, pl.ds(0, 3)], x.at[:, pl.ds(0, 3)], ysem_s, ysem_r.at[0], up).wait_send()
    weight = [1.0 / (jnp.full((1, 128), 1.0, F32) * (ends[i] - starts[i]).astype(F32)) for i in range(FR)]
    s1_all = rcopy(buf1.at[pl.ds(0, 7)], buf1.at[pl.ds(0, 7)], s1_s, s1_r, near_dev(1, 0))
    s1_all.wait_recv()

    parts = []
    for c in range(2):
        b = buf1[pl.ds(c * S, S)]
        tot = jnp.sum(b, axis=0)
        mean = tot * (1.0 / S)
        dm = b - mean[None]
        parts.append(jnp.where(lane == 0, mean, tot + 8192.0 * pltpu.roll(jnp.sum(dm * dm, axis=0), 1, 1)))
    chip_table = jnp.concatenate(parts, axis=0)
    ct[...] = chip_table
    buf2[2 * NX + cx] = chip_table

    s2 = {}
    for dz, dx in far:
        c = rcopy(ct, buf2.at[(2 - dz) * NX + cx], s2_s.at[dz + 2], s2_r.at[dz + 2], far_dev(dz, dx))
        s2.setdefault(dz, []).append(c)

    def start(dz):
        for c in s2[dz]:
            c.start()

    def whole(dz):
        part = buf2.at[pl.ds(0, len(s2[dz]))]
        return rcopy(part, part, s2_s.at[dz + 2], s2_r.at[dz + 2], near_dev(1, 0))

    def on(cond, act, *a):
        pl.when(cond)(lambda: act(*a))

    for dz in s2:
        on(has_z(dz), start, dz)
    s1_all.wait_send()
    for dz in s2:
        on(has_z(-dz), lambda dz: whole(dz).wait_recv(), dz)

    shape = (5 * NX, 8, 128)
    frame = ((cz - 2) * NX + lax.broadcasted_iota(jnp.int32, shape, 0)) * 8 + lax.broadcasted_iota(jnp.int32, shape, 1)
    entry = buf2[...]
    avgs, vs = [], []
    for i in range(FR):
        mask = ((frame >= starts[i]) & (frame < ends[i])).astype(F32)
        tot = jnp.sum(jnp.sum(mask * entry, axis=0), axis=0, keepdims=True) * weight[i]
        d = entry - tot[None]
        dd = jnp.sum(jnp.sum(mask * (d * d), axis=0), axis=0, keepdims=True) * weight[i]
        avgs.append(tot)
        vs.append(tot * (1.0 / 32768) + pltpu.roll(dd, 1, 1))
    both = jnp.concatenate(avgs + vs, axis=0)
    lane8 = lax.broadcasted_iota(jnp.int32, (8, 128), 1) % 4
    row8 = lax.broadcasted_iota(jnp.int32, (8, 128), 0)
    both = group_sum(jnp.where(lane8 == jnp.where(row8 < 4, 0, 1), both, 0.0))
    tab[...] = jnp.where(row8 < 4, both, lax.rsqrt(both + 1e-6))

    for dz in s2:
        on(has_z(dz), lambda dz: whole(dz).wait_send(), dz)


def norm_kernel(acc, tab, gain, shift, out, buf, sem):
    off = shift[...] * 0.5
    copies = []
    for c in range(8):
        i, p = c // 2, 2 * (c % 2)
        avg = tab[i : i + 1]
        scale = tab[i + 4 : i + 5] * gain[...] * 0.5
        for k in (p, p + 1):
            for h in range(2):
                v = (acc[i, k, :, h * 128 : (h + 1) * 128] - avg) * scale + off
                buf[i, 2 * k + h] = (v + v * jnp.tanh(v)).astype(BF)
        copies.append(pltpu.make_async_copy(buf.at[i, pl.ds(2 * p, 4)], out.at[i, pl.ds(2 * p, 4)], sem.at[c]))
        copies[-1].start()
    for c in copies:
        c.wait()


def shards(frames, conv_weight, norm_gain, norm_shift, clip_lengths):
    V = pltpu.VMEM

    def hbm(a):
        return pltpu.with_memory_space_constraint(a, pltpu.HBM)

    D = pltpu.SemaphoreType.DMA
    anyspec = pl.BlockSpec(memory_space=pltpu.HBM)
    vspec = pl.BlockSpec(memory_space=V)
    acc, tab = pl.pallas_call(
        conv_kernel,
        out_shape=(pltpu.VMEM((FR, 4, 256, 256), F32), pltpu.VMEM((8, 128), F32)),
        in_specs=[anyspec, anyspec, anyspec],
        out_specs=(vspec, vspec),
        scratch_shapes=[
            pltpu.SMEM((32,), jnp.int32),
            V((4, 8, 256, 128), BF), V((2, 8, 256, 128), BF), V((6, 256, 128), BF), V((6, 256, 128), BF),
            V((6, 5, 256, 768), BF), V((3, 1536, 256), BF),
            V((4, 4, 256), F32), V((4, 4, 256), F32), V((4, 128), F32), V((8, 128), F32),
            V((8, 4, 128), F32), V((20, 8, 128), F32),
            D, pltpu.SemaphoreType.REGULAR, pltpu.SemaphoreType.REGULAR,
            D((4,)), D((3,)), D, D((5,)), D, D((4,)), D, D, D((5,)), D((5,)),
        ],
        compiler_params=pltpu.CompilerParams(collective_id=0, has_side_effects=True, vmem_limit_bytes=56 * 2**20),
        name="conv_stats",
    )(hbm(frames), hbm(conv_weight), hbm(clip_lengths))
    return pl.pallas_call(
        norm_kernel,
        out_shape=jax.ShapeDtypeStruct((FR, ROWS, COLS, CH), BF),
        in_specs=[vspec, vspec, vspec, vspec],
        out_specs=anyspec,
        scratch_shapes=[V((FR, ROWS, COLS, CH), BF), D((8,))],
        compiler_params=pltpu.CompilerParams(vmem_limit_bytes=8 * 2**20),
        name="normalize",
    )(
        pltpu.with_memory_space_constraint(acc, V),
        pltpu.with_memory_space_constraint(tab, V),
        norm_gain.reshape(1, CH),
        norm_shift.reshape(1, CH),
    )


def solution(mesh):
    return jax.shard_map(
        shards,
        mesh=mesh,
        in_specs=(P("tm", "space", None, None), P(), P(), P(), P()),
        out_specs=P("tm", "space", None, None),
        check_vma=False,
    )
```

```python
import functools

import jax
import jax.numpy as jnp
from jax import lax
from jax.experimental import pallas as pl
from jax.experimental.pallas import tpu as pltpu
from jax.sharding import PartitionSpec as P

GROUPS = 32
MESH = pl.DeviceIdType.MESH
T, S, NX, NZ = 64, 4, 4, 8
FR, ROWS, COLS, CH = 4, 8, 256, 128
BF, F32 = jnp.bfloat16, jnp.float32


def shifted(v):
    z = jnp.zeros((1, CH), v.dtype)
    left = jnp.concatenate([z, v[: COLS - 1]], axis=0)
    right = jnp.concatenate([v[1:], z], axis=0)
    return jnp.concatenate([left, v, right], axis=1)


def group_sum(x):
    lane = lax.broadcasted_iota(jnp.int32, x.shape, 1)
    n = x.shape[1]
    x = x + jnp.where(lane % 2 == 0, pltpu.roll(x, n - 1, 1), pltpu.roll(x, 1, 1))
    return x + jnp.where(lane % 4 < 2, pltpu.roll(x, n - 2, 1), pltpu.roll(x, 2, 1))


def conv_kernel(x, w, lens_hbm, acc, tab, lens, XL, XH, YU, YD, PA, W, sS, sQ, st, ct, buf1, buf2,
                lensem, tok, tok2, lsem, wsem, xsem_s, xsem_r, ysem_s, ysem_r, s1_s, s1_r, s2_s, s2_r):
    t = lax.axis_index("tm")
    y = lax.axis_index("space")
    core = t % 2
    chip = t // 2
    cx = chip % NX
    cz = chip // NX

    def dev(z_, x_, c_, y_):
        return ((z_ * NX + x_) * 2 + c_, y_)

    nxt = ((t + 1) % T, y)
    up = (t, (y + 1) % S)
    down = (t, (y + S - 1) % S)

    near = [(dc, dy) for dc in range(2) for dy in (2, 1, 3, 0) if (dc, dy) != (0, 0)]
    far = [(dz, dx) for dz in (2, -2, 1, -1, 0) for dx in (2, 1, 3, 0) if (dz, dx) != (0, 0)]

    def near_dev(dc, dy):
        return dev(cz, cx, (core + dc) % 2, (y + dy) % S)

    def far_dev(dz, dx):
        return dev((cz + dz + NZ) % NZ, (cx + dx) % NX, core, y)

    has_next = t < T - 1
    has_prev = t > 0

    def has_z(dz):
        return (cz + dz >= 0) & (cz + dz < NZ)

    prev = ((t + T - 1) % T, y)
    direct = [(nxt, has_next), (up, None), (down, None), (prev, has_prev), (far_dev(0, 1), None), (far_dev(0, 3), None),
              (far_dev(1, 0), has_z(1)), (far_dev(-1, 0), has_z(-1))]
    second = [(far_dev(2, 0), has_z(2)), (far_dev(-2, 0), has_z(-2)), (far_dev(1, 0), has_z(1)), (far_dev(-1, 0), has_z(-1)),
              (near_dev(1, 0), None)]
    first = [(down, None), (far_dev(0, 3), None), (far_dev(1, 0), has_z(1)), (far_dev(-1, 0), has_z(-1))]
    barrier = pltpu.get_barrier_semaphore()

    def greet(sem, devices):
        for d, cond in devices:
            def signal(d=d):
                pl.semaphore_signal(sem, inc=1, device_id=d, device_id_type=MESH)
            if cond is None:
                signal()
            else:
                pl.when(cond)(signal)

    def count(devices):
        return sum(jnp.int32(1) if cond is None else cond.astype(jnp.int32) for _, cond in devices)

    loads = [pltpu.make_async_copy(x.at[f], XL.at[f], lsem.at[f]) for f in range(FR)]
    wloads = [pltpu.make_async_copy(w.at[lag], W.at[lag, pl.ds(0, 1152), pl.ds(0, 128)], wsem.at[lag]) for lag in range(3)]
    lens_load = pltpu.make_async_copy(lens_hbm, lens, lensem)
    for c in (lens_load, loads[0], wloads[0]):
        c.start()
    buf2[...] = jnp.zeros_like(buf2)
    greet(barrier, direct)
    for c in (loads[1], wloads[1], loads[2], wloads[2], loads[3]):
        c.start()
    for lag in range(3):
        W[lag, 1152:1536, 0:128] = jnp.zeros((384, 128), BF)
        W[lag, 0:384, 128:256] = jnp.zeros((384, 128), BF)

    pl.semaphore_wait(barrier, count(direct))

    def rcopy(src, dst, ss, rs, d):
        return pltpu.make_async_remote_copy(src_ref=src, dst_ref=dst, send_sem=ss, recv_sem=rs, device_id=d, device_id_type=MESH)

    xc = []
    for i, (r0, n) in enumerate([(0, 1), (7, 1), (1, 2), (3, 2), (5, 2)]):
        xc.append(rcopy(x.at[pl.ds(2, 2), pl.ds(r0, n)], XH.at[:, pl.ds(r0, n)], xsem_s, xsem_r.at[i], nxt))
    yc = [
        rcopy(x.at[:, 7], YU.at[pl.ds(2, 4)], ysem_s, ysem_r.at[0], up),
        rcopy(x.at[:, 0], YD.at[pl.ds(2, 4)], ysem_s, ysem_r.at[1], down),
        rcopy(XH.at[:, 7], YU.at[pl.ds(0, 2)], ysem_s, ysem_r.at[2], up),
        rcopy(XH.at[:, 0], YD.at[pl.ds(0, 2)], ysem_s, ysem_r.at[3], down),
    ]
    @pl.when(has_next)
    def _():
        xc[0].start()
        xc[1].start()

    yc[0].start()
    yc[1].start()

    @pl.when(has_next)
    def _():
        for c in xc[2:]:
            c.start()

    @pl.when(jnp.logical_not(has_prev))
    def _():
        XH[...] = jnp.zeros_like(XH)

    def landed(*copies):
        @pl.when(has_prev)
        def _():
            for c in copies:
                c.wait_recv()


    lens_load.wait()
    pos = [t * FR + i for i in range(FR)]

    def begin(k, c):
        cum, starts = c
        return cum + lens[k], tuple(jnp.where(cum <= p, cum, a) for p, a in zip(pos, starts))

    zero = jnp.int32(0)
    _, starts = lax.fori_loop(0, 32, begin, (zero, (zero,) * FR), unroll=4)
    within = [[jnp.where(pos[i] - lag >= starts[i], 1.0, 0.0).astype(F32) for lag in range(3)] for i in range(FR)]

    def build(f):
        for r in range(ROWS):
            e = r + 1
            PA[f + 2, e // 2, :, (e % 2) * 384 : (e % 2 + 1) * 384] = shifted(XL[f, r])

    def dot(a, b):
        return jnp.dot(a, b, preferred_element_type=F32)

    loads[0].wait()
    build(0)
    for f in range(FR):
        if f + 1 < FR:
            loads[f + 1].wait()
        if f < 3:
            wloads[f].wait()
            W[f, 384:1536, 128:256] = W[f, 0:1152, 0:128]
        tot = None
        for lag in range(min(f, 2), -1, -1):
            a = PA[f + 2 - lag, 1:4].reshape(768, 768)
            d1 = dot(a, W[lag, 768:1536])
            d0 = dot(a, W[lag, 0:768])
            if lag:
                d1 = d1 * within[f][lag]
                d0 = d0 * within[f][lag]
            tot = (d1, d0) if tot is None else (tot[0] + d1, tot[1] + d0)
        d1, d0 = tot[0].reshape(3, 256, 256), tot[1].reshape(3, 256, 256)
        acc[f, 0] = d1[0]
        acc[f, 1] = d1[1] + d0[0]
        acc[f, 2] = d1[2] + d0[1]
        acc[f, 3] = d0[2]
        if f + 1 < FR:
            build(f + 1)
        if f == 0:
            greet(tok, first)
        if f == 2:
            landed(xc[0], xc[1])
            yc[2].start()
            yc[3].start()
            pl.semaphore_wait(tok, count(first))
            greet(tok2, second)

    def stat(i, k):
        v = acc[i, k]
        s = jnp.sum(v, axis=0, keepdims=True)
        c = v - s * (1.0 / 256)
        q = jnp.sum(c * c, axis=0, keepdims=True)
        sS[i, k : k + 1] = s
        sQ[i, k : k + 1] = q

    has_up = y > 0
    has_down = y < S - 1
    yc[0].wait_recv()
    yc[1].wait_recv()
    zrow = jnp.zeros((COLS, CH), BF)

    def rims(f, _):
        PA[f, 0, :, 0:384] = shifted(jnp.where(has_up, YU[f], zrow))
        PA[f, 4, :, 384:768] = shifted(jnp.where(has_down, YD[f], zrow))
        return 0

    for f in range(2, 6):
        rims(f, 0)

    def rim_dots(lag, lo):
        n = FR - lo
        a = PA[lo + 2 - lag : FR + 2 - lag, 0].reshape(n * 256, 768)
        d = dot(a, W[lag, 0:768]).reshape(n, 256, 256)
        a2 = PA[lo + 2 - lag : FR + 2 - lag, 4].reshape(n * 256, 768)
        d2 = dot(a2, W[lag, 768:1536]).reshape(n, 256, 256)
        for i in range(lo, FR):
            acc[i, 0] += within[i][lag] * d[i - lo]
            acc[i, 3] += within[i][lag] * d2[i - lo]

    for lag in range(3):
        rim_dots(lag, lag)
    for i, k in ((2, 1), (2, 2), (3, 1), (3, 2)):
        stat(i, k)

    def early(p):
        a1 = PA[1, p]
        a2 = PA[0:2, p].reshape(512, 768)
        if p < 4:
            e = dot(a1, W[1, 0:768])
            g = dot(a2, W[2, 0:768])
            acc[0, p] += within[0][1] * e + within[0][2] * g[0:256]
            acc[1, p] += within[1][2] * g[256:512]
        if p > 0:
            e = dot(a1, W[1, 768:1536])
            g = dot(a2, W[2, 768:1536])
            acc[0, p - 1] += within[0][1] * e + within[0][2] * g[0:256]
            acc[1, p - 1] += within[1][2] * g[256:512]

    def early_rows(p):
        for f in range(2):
            PA[f, p, :, 0:384] = shifted(XH[f, 2 * p - 1])
            PA[f, p, :, 384:768] = shifted(XH[f, 2 * p])

    landed(xc[2])
    early_rows(1)
    early(1)
    for i, k in ((2, 0), (2, 3), (3, 0), (3, 3)):
        stat(i, k)
    yc[2].wait_recv()
    yc[3].wait_recv()
    for f in range(2):
        PA[f, 0, :, 384:768] = shifted(XH[f, 0])
        PA[f, 4, :, 0:384] = shifted(XH[f, 7])
    for f in range(2):
        rims(f, 0)
    early(0)
    early(4)
    landed(xc[3])
    early_rows(2)
    early(2)
    stat(0, 0)
    stat(1, 0)
    landed(xc[4])
    early_rows(3)
    early(3)
    for i, k in ((0, 1), (1, 1), (0, 2), (1, 2), (0, 3), (1, 3)):
        stat(i, k)

    lane = lax.broadcasted_iota(jnp.int32, (FR, 128), 1) % 4
    means, squares = [], []
    for i in range(FR):
        s = sS[i]
        m = s * (1.0 / 256)
        tot = jnp.sum(s, axis=0, keepdims=True)
        mean = (tot[:, :128] + tot[:, 128:]) * (1.0 / 2048)
        dm = m - jnp.concatenate([mean, mean], axis=1)
        qq = jnp.sum(sQ[i] + 256.0 * dm * dm, axis=0, keepdims=True)
        means.append(mean)
        squares.append(qq[:, :128] + qq[:, 128:])
    m = jnp.concatenate(means, axis=0)
    g = group_sum(m) * 0.25
    dm = m - g
    mine = jnp.where(lane == 0, g, group_sum(jnp.concatenate(squares, axis=0) + 2048.0 * dm * dm))
    st[...] = mine
    buf1[core * S + y] = mine

    s1 = []
    for dc, dy in near:
        s1.append(rcopy(st, buf1.at[core * S + y], s1_s, s1_r, near_dev(dc, dy)))
    pl.semaphore_wait(tok2, count(second))
    for c in s1:
        c.start()

    @pl.when(has_next)
    def _():
        rcopy(XH, XH, xsem_s, xsem_r.at[0], nxt).wait_send()

    rcopy(x.at[:, pl.ds(0, 3)], x.at[:, pl.ds(0, 3)], ysem_s, ysem_r.at[0], up).wait_send()
    def finish(k, c):
        cum, ends = c
        after = cum + lens[k]
        return after, tuple(jnp.where(cum <= p, after, a) for p, a in zip(pos, ends))

    _, ends = lax.fori_loop(0, 32, finish, (zero, (zero,) * FR), unroll=4)
    weight = [1.0 / (jnp.full((1, 128), 1.0, F32) * (ends[i] - starts[i]).astype(F32)) for i in range(FR)]
    s1_all = rcopy(buf1.at[pl.ds(0, 7)], buf1.at[pl.ds(0, 7)], s1_s, s1_r, near_dev(1, 0))
    s1_all.wait_recv()

    parts = []
    for c in range(2):
        b = buf1[pl.ds(c * S, S)]
        tot = jnp.sum(b, axis=0)
        mean = tot * (1.0 / S)
        dm = b - mean[None]
        parts.append(jnp.where(lane == 0, mean, tot + 8192.0 * pltpu.roll(jnp.sum(dm * dm, axis=0), 1, 1)))
    chip_table = jnp.concatenate(parts, axis=0)
    ct[...] = chip_table
    buf2[2 * NX + cx] = chip_table

    s2 = {}
    for dz, dx in far:
        c = rcopy(ct, buf2.at[(2 - dz) * NX + cx], s2_s.at[dz + 2], s2_r.at[dz + 2], far_dev(dz, dx))
        s2.setdefault(dz, []).append(c)

    def start(dz):
        for c in s2[dz]:
            c.start()

    def whole(dz):
        part = buf2.at[pl.ds(0, len(s2[dz]))]
        return rcopy(part, part, s2_s.at[dz + 2], s2_r.at[dz + 2], near_dev(1, 0))

    def on(cond, act, *a):
        pl.when(cond)(lambda: act(*a))

    for dz in s2:
        on(has_z(dz), start, dz)
    s1_all.wait_send()
    for dz in s2:
        on(has_z(dz), lambda dz: whole(dz).wait_send(), dz)
    for dz in s2:
        on(has_z(-dz), lambda dz: whole(dz).wait_recv(), dz)

    shape = (5 * NX, 8, 128)
    frame = ((cz - 2) * NX + lax.broadcasted_iota(jnp.int32, shape, 0)) * 8 + lax.broadcasted_iota(jnp.int32, shape, 1)
    entry = buf2[...]
    avgs, vs = [], []
    for i in range(FR):
        mask = ((frame >= starts[i]) & (frame < ends[i])).astype(F32)
        tot = jnp.sum(jnp.sum(mask * entry, axis=0), axis=0, keepdims=True) * weight[i]
        d = entry - tot[None]
        dd = jnp.sum(jnp.sum(mask * (d * d), axis=0), axis=0, keepdims=True) * weight[i]
        avgs.append(tot)
        vs.append(tot * (1.0 / 32768) + pltpu.roll(dd, 1, 1))
    both = jnp.concatenate(avgs + vs, axis=0)
    lane8 = lax.broadcasted_iota(jnp.int32, (8, 128), 1) % 4
    row8 = lax.broadcasted_iota(jnp.int32, (8, 128), 0)
    both = group_sum(jnp.where(lane8 == jnp.where(row8 < 4, 0, 1), both, 0.0))
    tab[...] = jnp.where(row8 < 4, both, lax.rsqrt(both + 1e-6))


def norm_kernel(acc, tab, gain, shift, out, buf, sem):
    off = shift[...] * 0.5
    copies = []
    for c in range(8):
        i, p = c // 2, 2 * (c % 2)
        avg = tab[i : i + 1]
        scale = tab[i + 4 : i + 5] * gain[...] * 0.5
        for k in (p, p + 1):
            for h in range(2):
                v = (acc[i, k, :, h * 128 : (h + 1) * 128] - avg) * scale + off
                buf[i, 2 * k + h] = (v + v * jnp.tanh(v)).astype(BF)
        copies.append(pltpu.make_async_copy(buf.at[i, pl.ds(2 * p, 4)], out.at[i, pl.ds(2 * p, 4)], sem.at[c]))
        copies[-1].start()
    for c in copies:
        c.wait()


def shards(frames, conv_weight, norm_gain, norm_shift, clip_lengths):
    V = pltpu.VMEM

    def hbm(a):
        return pltpu.with_memory_space_constraint(a, pltpu.HBM)

    D = pltpu.SemaphoreType.DMA
    anyspec = pl.BlockSpec(memory_space=pltpu.HBM)
    vspec = pl.BlockSpec(memory_space=V)
    acc, tab = pl.pallas_call(
        conv_kernel,
        out_shape=(pltpu.VMEM((FR, 4, 256, 256), F32), pltpu.VMEM((8, 128), F32)),
        in_specs=[anyspec, anyspec, anyspec],
        out_specs=(vspec, vspec),
        scratch_shapes=[
            pltpu.SMEM((32,), jnp.int32),
            V((4, 8, 256, 128), BF), V((2, 8, 256, 128), BF), V((6, 256, 128), BF), V((6, 256, 128), BF),
            V((6, 5, 256, 768), BF), V((3, 1536, 256), BF),
            V((4, 4, 256), F32), V((4, 4, 256), F32), V((4, 128), F32), V((8, 128), F32),
            V((8, 4, 128), F32), V((20, 8, 128), F32),
            D, pltpu.SemaphoreType.REGULAR, pltpu.SemaphoreType.REGULAR,
            D((4,)), D((3,)), D, D((5,)), D, D((4,)), D, D, D((5,)), D((5,)),
        ],
        compiler_params=pltpu.CompilerParams(collective_id=0, has_side_effects=True, vmem_limit_bytes=56 * 2**20),
        name="conv_stats",
    )(hbm(frames), hbm(conv_weight), hbm(clip_lengths))
    return pl.pallas_call(
        norm_kernel,
        out_shape=jax.ShapeDtypeStruct((FR, ROWS, COLS, CH), BF),
        in_specs=[vspec, vspec, vspec, vspec],
        out_specs=anyspec,
        scratch_shapes=[V((FR, ROWS, COLS, CH), BF), D((8,))],
        compiler_params=pltpu.CompilerParams(vmem_limit_bytes=8 * 2**20),
        name="normalize",
    )(
        pltpu.with_memory_space_constraint(acc, V),
        pltpu.with_memory_space_constraint(tab, V),
        norm_gain.reshape(1, CH),
        norm_shift.reshape(1, CH),
    )


def solution(mesh):
    return jax.shard_map(
        shards,
        mesh=mesh,
        in_specs=(P("tm", "space", None, None), P(), P(), P(), P()),
        out_specs=P("tm", "space", None, None),
        check_vma=False,
    )
```

```python
import functools

import jax
import jax.numpy as jnp
from jax import lax
from jax.experimental import pallas as pl
from jax.experimental.pallas import tpu as pltpu
from jax.sharding import PartitionSpec as P

GROUPS = 32
MESH = pl.DeviceIdType.MESH
T, S, NX, NZ = 64, 4, 4, 8
FR, ROWS, COLS, CH = 4, 8, 256, 128
BF, F32 = jnp.bfloat16, jnp.float32


def shifted(v):
    z = jnp.zeros((1, CH), v.dtype)
    left = jnp.concatenate([z, v[: COLS - 1]], axis=0)
    right = jnp.concatenate([v[1:], z], axis=0)
    return jnp.concatenate([left, v, right], axis=1)


def group_sum(x):
    lane = lax.broadcasted_iota(jnp.int32, x.shape, 1)
    n = x.shape[1]
    x = x + jnp.where(lane % 2 == 0, pltpu.roll(x, n - 1, 1), pltpu.roll(x, 1, 1))
    return x + jnp.where(lane % 4 < 2, pltpu.roll(x, n - 2, 1), pltpu.roll(x, 2, 1))


def conv_kernel(x, w, lens_hbm, acc, tab, lens, XL, XH, YU, YD, PA, W, sS, sQ, st, ct, buf1, buf2,
                lensem, tok, tok2, lsem, wsem, xsem_s, xsem_r, ysem_s, ysem_r, s1_s, s1_r, s2_s, s2_r):
    t = lax.axis_index("tm")
    y = lax.axis_index("space")
    core = t % 2
    chip = t // 2
    cx = chip % NX
    cz = chip // NX

    def dev(z_, x_, c_, y_):
        return ((z_ * NX + x_) * 2 + c_, y_)

    nxt = ((t + 1) % T, y)
    up = (t, (y + 1) % S)
    down = (t, (y + S - 1) % S)

    near = [(dc, dy) for dc in range(2) for dy in (2, 1, 3, 0) if (dc, dy) != (0, 0)]
    far = [(dz, dx) for dz in (2, -2, 1, -1, 0) for dx in (2, 1, 3, 0) if (dz, dx) != (0, 0)]

    def near_dev(dc, dy):
        return dev(cz, cx, (core + dc) % 2, (y + dy) % S)

    def far_dev(dz, dx):
        return dev((cz + dz + NZ) % NZ, (cx + dx) % NX, core, y)

    has_next = t < T - 1
    has_prev = t > 0

    def has_z(dz):
        return (cz + dz >= 0) & (cz + dz < NZ)

    prev = ((t + T - 1) % T, y)
    direct = [(nxt, has_next), (up, None), (down, None), (prev, has_prev), (far_dev(0, 1), None), (far_dev(0, 3), None),
              (far_dev(1, 0), has_z(1)), (far_dev(-1, 0), has_z(-1))]
    second = [(far_dev(2, 0), has_z(2)), (far_dev(-2, 0), has_z(-2)), (far_dev(1, 0), has_z(1)), (far_dev(-1, 0), has_z(-1)),
              (near_dev(1, 0), None)]
    first = [(down, None), (far_dev(0, 3), None), (far_dev(1, 0), has_z(1)), (far_dev(-1, 0), has_z(-1))]
    barrier = pltpu.get_barrier_semaphore()

    def greet(sem, devices):
        for d, cond in devices:
            def signal(d=d):
                pl.semaphore_signal(sem, inc=1, device_id=d, device_id_type=MESH)
            if cond is None:
                signal()
            else:
                pl.when(cond)(signal)

    def count(devices):
        return sum(jnp.int32(1) if cond is None else cond.astype(jnp.int32) for _, cond in devices)

    loads = [pltpu.make_async_copy(x.at[f], XL.at[f], lsem.at[f]) for f in range(FR)]
    wloads = [pltpu.make_async_copy(w.at[lag], W.at[lag, pl.ds(0, 1152), pl.ds(0, 128)], wsem.at[lag]) for lag in range(3)]
    lens_load = pltpu.make_async_copy(lens_hbm, lens, lensem)
    for c in (lens_load, loads[0], wloads[0]):
        c.start()
    buf2[...] = jnp.zeros_like(buf2)
    greet(barrier, direct)
    for c in (loads[1], wloads[1], loads[2], wloads[2], loads[3]):
        c.start()
    for lag in range(3):
        W[lag, 1152:1536, 0:128] = jnp.zeros((384, 128), BF)
        W[lag, 0:384, 128:256] = jnp.zeros((384, 128), BF)

    pl.semaphore_wait(barrier, count(direct))

    def rcopy(src, dst, ss, rs, d):
        return pltpu.make_async_remote_copy(src_ref=src, dst_ref=dst, send_sem=ss, recv_sem=rs, device_id=d, device_id_type=MESH)

    xc = []
    for i, (r0, n) in enumerate([(0, 1), (7, 1), (1, 2), (3, 2), (5, 2)]):
        xc.append(rcopy(x.at[pl.ds(2, 2), pl.ds(r0, n)], XH.at[:, pl.ds(r0, n)], xsem_s, xsem_r.at[i], nxt))
    yc = [
        rcopy(x.at[:, 7], YU.at[pl.ds(2, 4)], ysem_s, ysem_r.at[0], up),
        rcopy(x.at[:, 0], YD.at[pl.ds(2, 4)], ysem_s, ysem_r.at[1], down),
        rcopy(XH.at[:, 7], YU.at[pl.ds(0, 2)], ysem_s, ysem_r.at[2], up),
        rcopy(XH.at[:, 0], YD.at[pl.ds(0, 2)], ysem_s, ysem_r.at[3], down),
    ]
    @pl.when(has_next)
    def _():
        xc[0].start()
        xc[1].start()

    yc[0].start()
    yc[1].start()

    @pl.when(has_next)
    def _():
        for c in xc[2:]:
            c.start()

    @pl.when(jnp.logical_not(has_prev))
    def _():
        XH[...] = jnp.zeros_like(XH)

    def landed(*copies):
        @pl.when(has_prev)
        def _():
            for c in copies:
                c.wait_recv()


    lens_load.wait()
    pos = [t * FR + i for i in range(FR)]

    def begin(k, c):
        cum, starts = c
        return cum + lens[k], tuple(jnp.where(cum <= p, cum, a) for p, a in zip(pos, starts))

    zero = jnp.int32(0)
    _, starts = lax.fori_loop(0, 32, begin, (zero, (zero,) * FR), unroll=4)
    within = [[jnp.where(pos[i] - lag >= starts[i], 1.0, 0.0).astype(F32) for lag in range(3)] for i in range(FR)]

    def build(f):
        for r in range(ROWS):
            e = r + 1
            PA[f + 2, e // 2, :, (e % 2) * 384 : (e % 2 + 1) * 384] = shifted(XL[f, r])

    def dot(a, b):
        return jnp.dot(a, b, preferred_element_type=F32)

    loads[0].wait()
    build(0)
    for f in range(FR):
        if f + 1 < FR:
            loads[f + 1].wait()
        if f < 3:
            wloads[f].wait()
            W[f, 384:1536, 128:256] = W[f, 0:1152, 0:128]
        tot = None
        for lag in range(min(f, 2), -1, -1):
            a = PA[f + 2 - lag, 1:4].reshape(768, 768)
            d1 = dot(a, W[lag, 768:1536])
            d0 = dot(a, W[lag, 0:768])
            if lag:
                d1 = d1 * within[f][lag]
                d0 = d0 * within[f][lag]
            tot = (d1, d0) if tot is None else (tot[0] + d1, tot[1] + d0)
        d1, d0 = tot[0].reshape(3, 256, 256), tot[1].reshape(3, 256, 256)
        acc[f, 0] = d1[0]
        acc[f, 1] = d1[1] + d0[0]
        acc[f, 2] = d1[2] + d0[1]
        acc[f, 3] = d0[2]
        if f + 1 < FR:
            build(f + 1)
        if f == 0:
            greet(tok, first)
        if f == 2:
            landed(xc[0], xc[1])
            yc[2].start()
            yc[3].start()
            pl.semaphore_wait(tok, count(first))
            greet(tok2, second)

    def stat(i, k):
        v = acc[i, k]
        s = jnp.sum(v, axis=0, keepdims=True)
        c = v - s * (1.0 / 256)
        q = jnp.sum(c * c, axis=0, keepdims=True)
        sS[i, k : k + 1] = s
        sQ[i, k : k + 1] = q

    has_up = y > 0
    has_down = y < S - 1
    yc[0].wait_recv()
    yc[1].wait_recv()
    zrow = jnp.zeros((COLS, CH), BF)

    def rims(f, _):
        PA[f, 0, :, 0:384] = shifted(jnp.where(has_up, YU[f], zrow))
        PA[f, 4, :, 384:768] = shifted(jnp.where(has_down, YD[f], zrow))
        return 0

    for f in range(2, 6):
        rims(f, 0)

    def rim_dots(lag, lo):
        n = FR - lo
        a = PA[lo + 2 - lag : FR + 2 - lag, 0].reshape(n * 256, 768)
        d = dot(a, W[lag, 0:768]).reshape(n, 256, 256)
        a2 = PA[lo + 2 - lag : FR + 2 - lag, 4].reshape(n * 256, 768)
        d2 = dot(a2, W[lag, 768:1536]).reshape(n, 256, 256)
        for i in range(lo, FR):
            acc[i, 0] += within[i][lag] * d[i - lo]
            acc[i, 3] += within[i][lag] * d2[i - lo]

    for lag in range(3):
        rim_dots(lag, lag)
    for i, k in ((2, 1), (2, 2), (3, 1), (3, 2)):
        stat(i, k)

    def early(p):
        a1 = PA[1, p]
        a2 = PA[0:2, p].reshape(512, 768)
        if p < 4:
            e = dot(a1, W[1, 0:768])
            g = dot(a2, W[2, 0:768])
            acc[0, p] += within[0][1] * e + within[0][2] * g[0:256]
            acc[1, p] += within[1][2] * g[256:512]
        if p > 0:
            e = dot(a1, W[1, 768:1536])
            g = dot(a2, W[2, 768:1536])
            acc[0, p - 1] += within[0][1] * e + within[0][2] * g[0:256]
            acc[1, p - 1] += within[1][2] * g[256:512]

    def early_rows(p):
        for f in range(2):
            PA[f, p, :, 0:384] = shifted(XH[f, 2 * p - 1])
            PA[f, p, :, 384:768] = shifted(XH[f, 2 * p])

    landed(xc[2])
    early_rows(1)
    early(1)
    for i, k in ((2, 0), (2, 3), (3, 0), (3, 3)):
        stat(i, k)
    yc[2].wait_recv()
    yc[3].wait_recv()
    for f in range(2):
        PA[f, 0, :, 384:768] = shifted(XH[f, 0])
        PA[f, 4, :, 0:384] = shifted(XH[f, 7])
    for f in range(2):
        rims(f, 0)
    early(0)
    early(4)
    stat(0, 0)
    stat(1, 0)
    landed(xc[3])
    early_rows(2)
    early(2)
    stat(0, 1)
    stat(1, 1)
    landed(xc[4])
    early_rows(3)
    early(3)
    for i, k in ((0, 2), (1, 2), (0, 3), (1, 3)):
        stat(i, k)

    lane = lax.broadcasted_iota(jnp.int32, (FR, 128), 1) % 4
    means, squares = [], []
    for i in range(FR):
        s = sS[i]
        m = s * (1.0 / 256)
        tot = jnp.sum(s, axis=0, keepdims=True)
        mean = (tot[:, :128] + tot[:, 128:]) * (1.0 / 2048)
        dm = m - jnp.concatenate([mean, mean], axis=1)
        qq = jnp.sum(sQ[i] + 256.0 * dm * dm, axis=0, keepdims=True)
        means.append(mean)
        squares.append(qq[:, :128] + qq[:, 128:])
    m = jnp.concatenate(means, axis=0)
    g = group_sum(m) * 0.25
    dm = m - g
    mine = jnp.where(lane == 0, g, group_sum(jnp.concatenate(squares, axis=0) + 2048.0 * dm * dm))
    st[...] = mine
    buf1[core * S + y] = mine

    s1 = []
    for dc, dy in near:
        s1.append(rcopy(st, buf1.at[core * S + y], s1_s, s1_r, near_dev(dc, dy)))
    pl.semaphore_wait(tok2, count(second))
    for c in s1:
        c.start()

    @pl.when(has_next)
    def _():
        rcopy(XH, XH, xsem_s, xsem_r.at[0], nxt).wait_send()

    rcopy(x.at[:, pl.ds(0, 3)], x.at[:, pl.ds(0, 3)], ysem_s, ysem_r.at[0], up).wait_send()
    def finish(k, c):
        cum, ends = c
        after = cum + lens[k]
        return after, tuple(jnp.where(cum <= p, after, a) for p, a in zip(pos, ends))

    _, ends = lax.fori_loop(0, 32, finish, (zero, (zero,) * FR), unroll=4)
    weight = [1.0 / (jnp.full((1, 128), 1.0, F32) * (ends[i] - starts[i]).astype(F32)) for i in range(FR)]
    s1_all = rcopy(buf1.at[pl.ds(0, 7)], buf1.at[pl.ds(0, 7)], s1_s, s1_r, near_dev(1, 0))
    s1_all.wait_recv()

    parts = []
    for c in range(2):
        b = buf1[pl.ds(c * S, S)]
        tot = jnp.sum(b, axis=0)
        mean = tot * (1.0 / S)
        dm = b - mean[None]
        parts.append(jnp.where(lane == 0, mean, tot + 8192.0 * pltpu.roll(jnp.sum(dm * dm, axis=0), 1, 1)))
    chip_table = jnp.concatenate(parts, axis=0)
    ct[...] = chip_table
    buf2[2 * NX + cx] = chip_table

    s2 = {}
    for dz, dx in far:
        c = rcopy(ct, buf2.at[(2 - dz) * NX + cx], s2_s.at[dz + 2], s2_r.at[dz + 2], far_dev(dz, dx))
        s2.setdefault(dz, []).append(c)

    def start(dz):
        for c in s2[dz]:
            c.start()

    def whole(dz):
        part = buf2.at[pl.ds(0, len(s2[dz]))]
        return rcopy(part, part, s2_s.at[dz + 2], s2_r.at[dz + 2], near_dev(1, 0))

    def on(cond, act, *a):
        pl.when(cond)(lambda: act(*a))

    for dz in s2:
        on(has_z(dz), start, dz)
    s1_all.wait_send()
    for dz in s2:
        on(has_z(dz), lambda dz: whole(dz).wait_send(), dz)
    for dz in s2:
        on(has_z(-dz), lambda dz: whole(dz).wait_recv(), dz)

    shape = (5 * NX, 8, 128)
    frame = ((cz - 2) * NX + lax.broadcasted_iota(jnp.int32, shape, 0)) * 8 + lax.broadcasted_iota(jnp.int32, shape, 1)
    entry = buf2[...]
    avgs, vs = [], []
    for i in range(FR):
        mask = ((frame >= starts[i]) & (frame < ends[i])).astype(F32)
        tot = jnp.sum(jnp.sum(mask * entry, axis=0), axis=0, keepdims=True) * weight[i]
        d = entry - tot[None]
        dd = jnp.sum(jnp.sum(mask * (d * d), axis=0), axis=0, keepdims=True) * weight[i]
        avgs.append(tot)
        vs.append(tot * (1.0 / 32768) + pltpu.roll(dd, 1, 1))
    both = jnp.concatenate(avgs + vs, axis=0)
    lane8 = lax.broadcasted_iota(jnp.int32, (8, 128), 1) % 4
    row8 = lax.broadcasted_iota(jnp.int32, (8, 128), 0)
    both = group_sum(jnp.where(lane8 == jnp.where(row8 < 4, 0, 1), both, 0.0))
    tab[...] = jnp.where(row8 < 4, both, lax.rsqrt(both + 1e-6))


def norm_kernel(acc, tab, gain, shift, out, buf, sem):
    off = shift[...] * 0.5
    copies = []
    for c in range(8):
        i, p = c // 2, 2 * (c % 2)
        avg = tab[i : i + 1]
        scale = tab[i + 4 : i + 5] * gain[...] * 0.5
        for k in (p, p + 1):
            for h in range(2):
                v = (acc[i, k, :, h * 128 : (h + 1) * 128] - avg) * scale + off
                buf[i, 2 * k + h] = (v + v * jnp.tanh(v)).astype(BF)
        copies.append(pltpu.make_async_copy(buf.at[i, pl.ds(2 * p, 4)], out.at[i, pl.ds(2 * p, 4)], sem.at[c]))
        copies[-1].start()
    for c in copies:
        c.wait()


def shards(frames, conv_weight, norm_gain, norm_shift, clip_lengths):
    V = pltpu.VMEM

    def hbm(a):
        return pltpu.with_memory_space_constraint(a, pltpu.HBM)

    D = pltpu.SemaphoreType.DMA
    anyspec = pl.BlockSpec(memory_space=pltpu.HBM)
    vspec = pl.BlockSpec(memory_space=V)
    acc, tab = pl.pallas_call(
        conv_kernel,
        out_shape=(pltpu.VMEM((FR, 4, 256, 256), F32), pltpu.VMEM((8, 128), F32)),
        in_specs=[anyspec, anyspec, anyspec],
        out_specs=(vspec, vspec),
        scratch_shapes=[
            pltpu.SMEM((32,), jnp.int32),
            V((4, 8, 256, 128), BF), V((2, 8, 256, 128), BF), V((6, 256, 128), BF), V((6, 256, 128), BF),
            V((6, 5, 256, 768), BF), V((3, 1536, 256), BF),
            V((4, 4, 256), F32), V((4, 4, 256), F32), V((4, 128), F32), V((8, 128), F32),
            V((8, 4, 128), F32), V((20, 8, 128), F32),
            D, pltpu.SemaphoreType.REGULAR, pltpu.SemaphoreType.REGULAR,
            D((4,)), D((3,)), D, D((5,)), D, D((4,)), D, D, D((5,)), D((5,)),
        ],
        compiler_params=pltpu.CompilerParams(collective_id=0, has_side_effects=True, vmem_limit_bytes=56 * 2**20),
        name="conv_stats",
    )(hbm(frames), hbm(conv_weight), hbm(clip_lengths))
    return pl.pallas_call(
        norm_kernel,
        out_shape=jax.ShapeDtypeStruct((FR, ROWS, COLS, CH), BF),
        in_specs=[vspec, vspec, vspec, vspec],
        out_specs=anyspec,
        scratch_shapes=[V((FR, ROWS, COLS, CH), BF), D((8,))],
        compiler_params=pltpu.CompilerParams(vmem_limit_bytes=8 * 2**20),
        name="normalize",
    )(
        pltpu.with_memory_space_constraint(acc, V),
        pltpu.with_memory_space_constraint(tab, V),
        norm_gain.reshape(1, CH),
        norm_shift.reshape(1, CH),
    )


def solution(mesh):
    return jax.shard_map(
        shards,
        mesh=mesh,
        in_specs=(P("tm", "space", None, None), P(), P(), P(), P()),
        out_specs=P("tm", "space", None, None),
        check_vma=False,
    )
```
